128 devices in a mesh: frames: 4 (over y_lo, core), hidden: 32 (over y_hi, x, z).
Axes of the slice: x: 4, y: 4 (y_hi: 2, y_lo: 2; y = y_hi * 2 + y_lo), z: 4, core: 2. Of those that a mesh axis runs over, the one named last changes fastest.
Arguments:
- frames_in: bfloat16 [2048, 2048], P('frames', 'hidden'), may hold values from -6 to 6
- in_gain: float32 [2048], replicated, may hold values from 0.1 to 1.9
- w_in: bfloat16 [2048, 8192], P(None, 'hidden'), may hold values from -0.125 to 0.125
- w_out: bfloat16 [8192, 2048], P('hidden'), may hold values from -0.0625 to 0.0625
- out_gain: float32 [2048], replicated, may hold values from 0.1 to 1.9
- table: bfloat16 [151936, 2048], P(('frames', 'hidden')), may hold values from -8 to 8
Outputs:
- soft_embed: bfloat16 [2048, 2048], P('frames', 'hidden')
- log_total: float32 [2048], P('frames')
The draws below stay inside these ranges and needn't reach their ends.
All inputs are finite; a program needn't handle non-finite values.
Results may differ from the reference program's by a relative error of at most 0.0085.
The reference program's roundings to bfloat16 on the way (of `normed`, `hidden`, `latent` and `weights`) count: a program that leaves them out, or rounds other values in their place, can miss the bound.
Values may be sent and summed in bfloat16 or wider, within the bound.
A program may use at most 128 MiB of HBM per device.

```python
import math
import jax
import jax.numpy as jnp
from jax import lax

D = 2048
FF = 8192
V = 151936
FRAMES = 2048


def shared_frames(key):
    return jnp.clip(jax.random.normal(key, (FRAMES, D), jnp.float32), -6.0, 6.0)


def draw_frames_in(key, part):
    return shared_frames(key).astype(jnp.bfloat16)


def draw_table(key, part):
    key = jax.random.fold_in(key, 7)
    value_key = jax.random.fold_in(key, 1)
    entries = jnp.clip(jax.random.normal(value_key, (V, D), jnp.float32), -8.0, 8.0)
    return entries.astype(jnp.bfloat16)


def shard_levels(key, shape, cuts, smallest, largest):
    gain = 1.0
    for dim, shards_of in cuts:
        steps = jax.random.uniform(jax.random.fold_in(jax.random.fold_in(key, 6), dim), (shards_of,), jnp.float32, smallest / len(cuts), largest / len(cuts))
        gain = gain * jnp.repeat(jnp.exp(steps), shape[dim] // shards_of).reshape((-1,) + (1,) * (len(shape) - 1 - dim))
    return gain


def bell_draw(stream_key, shape, spread, limit, shards=(), dtype=jnp.bfloat16):
    array = jax.random.normal(stream_key, shape, jnp.float32) * spread
    if len(shards) > 0:
        array = shard_levels(stream_key, shape, shards, -0.22, 0.18) * array
    return jnp.clip(array, min=-limit, max=limit).astype(dtype)


def setup_inputs(seed: int = 0) -> dict:
    key_list = jax.random.split(jax.random.key(seed), 7)
    return {
        "frames_in": draw_frames_in(jax.random.fold_in(key_list[6], 71), 0),
        "in_gain": jnp.clip(1.0 + 0.18 * jax.random.normal(key_list[1], (D,), jnp.float32), 0.1, 1.9),
        "w_in": bell_draw(key_list[2], (D, FF), D ** -0.5, 0.125, ((1, 32),)),
        "w_out": bell_draw(key_list[3], (FF, D), FF ** -0.5, 0.0625, ((0, 32),)),
        "out_gain": jnp.clip(1.0 + 0.18 * jax.random.normal(key_list[4], (D,), jnp.float32), 0.1, 1.9),
        "table": draw_table(jax.random.fold_in(key_list[6], 71), 0),
    }


def rms_scale(values, gain_vec):
    mean_sq = lax.optimization_barrier(jnp.mean(values * values, axis=-1, keepdims=True))
    return values * lax.rsqrt(mean_sq + 1e-06) * gain_vec

def reference(frames_in, in_gain, w_in, w_out, out_gain, table):
    inputs = frames_in.astype(jnp.float32)
    normed = rms_scale(inputs, in_gain).astype(jnp.bfloat16)
    hidden = jax.nn.gelu(jnp.dot(normed, w_in, preferred_element_type=jnp.float32), approximate=True).astype(jnp.bfloat16)
    encoded = inputs + jnp.dot(hidden, w_out, preferred_element_type=jnp.float32)
    latent = rms_scale(encoded, out_gain).astype(jnp.bfloat16)
    score_scale = 5.0 / math.sqrt(D)

    def score_block(frame_block):
        scores = jnp.dot(frame_block, table.T, preferred_element_type=jnp.float32) * score_scale
        highest = lax.optimization_barrier(jnp.max(scores, axis=1))
        exponent = jnp.exp(scores - highest[:, None])
        row_total = lax.optimization_barrier(jnp.sum(exponent, axis=1))
        weights = exponent.astype(jnp.bfloat16)
        mixed = jnp.dot(weights, table, preferred_element_type=jnp.float32) / row_total[:, None]
        return (mixed.astype(jnp.bfloat16), highest + jnp.log(row_total))
    blocked = latent.reshape(FRAMES // 128, 128, D)
    soft_embed, log_total = lax.map(score_block, blocked)
    return (soft_embed.reshape(FRAMES, D), log_total.reshape(FRAMES))
```

```python
import functools
import math

import jax
import jax.numpy as jnp
from jax import lax
from jax.experimental import pallas as pl
from jax.experimental.pallas import tpu as pltpu
from jax.sharding import PartitionSpec as P

MESH = pl.DeviceIdType.MESH
D = 2048
ROWS = 1187
HALF = 1216
VP = 2 * HALF
VT = 608
F32 = jnp.float32
BF16 = jnp.bfloat16
ALL = slice(None)


def coords():
    f = lax.axis_index("frames")
    h = lax.axis_index("hidden")
    return {
        "x": lax.rem(lax.div(h, 4), 4),
        "y": lax.div(h, 16) * 2 + lax.div(f, 2),
        "z": lax.rem(h, 4),
        "c": lax.rem(f, 2),
    }


def device(at):
    return (
        lax.rem(at["y"], 2) * 2 + at["c"],
        lax.div(at["y"], 2) * 16 + at["x"] * 4 + at["z"],
    )


def moved(me, dim, by):
    return device({**me, dim: lax.rem(me[dim] + by + 4, 4)})


class Links:
    def __init__(self, send_sems, recv_sems):
        self.send_sems, self.recv_sems, self.copies = send_sems, recv_sems, []

    def send(self, src, dst, to):
        k = len(self.copies)
        copy = pltpu.make_async_remote_copy(
            src_ref=src,
            dst_ref=dst,
            send_sem=self.send_sems.at[k],
            recv_sem=self.recv_sems.at[k],
            device_id=to,
            device_id_type=MESH,
        )
        copy.start()
        self.copies.append(copy)
        return copy

    def drain(self):
        for copy in self.copies:
            copy.wait_send()


def run(*streams):
    streams = list(streams)
    while streams:
        for stream in list(streams):
            try:
                next(stream)
            except StopIteration:
                streams.remove(stream)


def ring_gather(links, me, dim, view, low, high):
    i = me[dim]
    right, left = moved(me, dim, 1), moved(me, dim, -1)
    before, after = lax.rem(i + 3, 4), lax.rem(i + 1, 4)
    r_low = links.send(view(i, low), view(i, low), right)
    l_high = links.send(view(i, high), view(i, high), left)
    r_high = links.send(view(i, high), view(i, high), right)
    l_low = links.send(view(i, low), view(i, low), left)
    yield
    r_low.wait_recv()
    r_far = links.send(view(before, low), view(before, low), right)
    l_high.wait_recv()
    l_far = links.send(view(after, high), view(after, high), left)
    yield
    r_high.wait_recv()
    l_low.wait_recv()
    r_far.wait_recv()
    l_far.wait_recv()


def ring_reduce(links, me, dim, view, near, far, low, high, add):
    i = me[dim]
    right, left = moved(me, dim, 1), moved(me, dim, -1)
    before, after, across = lax.rem(i + 3, 4), lax.rem(i + 1, 4), lax.rem(i + 2, 4)
    r_far = links.send(view(across, low), far[0](low), right)
    l_far = links.send(view(across, high), far[1](high), left)
    r_high = links.send(view(after, high), near[0](high), right)
    l_low = links.send(view(before, low), near[1](low), left)
    yield
    r_far.wait_recv()
    add(after, low, [far[0]])
    r_low = links.send(view(after, low), near[0](low), right)
    l_far.wait_recv()
    add(before, high, [far[1]])
    l_high = links.send(view(before, high), near[1](high), left)
    yield
    r_high.wait_recv()
    l_high.wait_recv()
    add(i, high, [near[0], near[1]])
    l_low.wait_recv()
    r_low.wait_recv()
    add(i, low, [near[0], near[1]])


def greet(peers):
    barrier = pltpu.get_barrier_semaphore()
    for peer in peers:
        pl.semaphore_signal(barrier, inc=1, device_id=peer, device_id_type=MESH)
    pl.semaphore_wait(barrier, len(peers))


def ffn_lead(sel):
    return tuple(ALL if sel[d] is None else sel[d] for d in ("w", "x", "z"))


def ffn_kernel(
    x_ref, gin_ref, win_ref, wout_ref, gout_ref, lat_ref,
    xb, xs, part, far_a, near_a, far_b, near_b, far_c, near_c, far_d, near_d, wrecv, ssem, rsem,
):
    me = coords()
    me_w = lax.div(me["y"], 2)
    opposite = moved(me, "y", 2)
    greet(
        [moved(me, "x", 1), moved(me, "x", -1), moved(me, "z", 1), moved(me, "z", -1), opposite]
    )
    links = Links(ssem, rsem)
    xb[me_w, me["x"], me["z"]] = x_ref[...]

    def gather(k, order):
        rows = (pl.ds(128 * k, 64), pl.ds(128 * k + 64, 64))
        whole = pl.ds(128 * k, 128)
        mine = xb.at[me_w, me["x"], me["z"], whole]
        across = links.send(mine, mine, opposite)
        yield
        across.wait_recv()
        sel = {"w": None, "x": me["x"], "z": me["z"]}
        for dim in order:
            def view(i, r, dim=dim, sel=dict(sel)):
                return xb.at[(*ffn_lead({**sel, dim: i}), r)]
            yield from ring_gather(links, me, dim, view, *rows)
            sel[dim] = None

    run(gather(0, "xz"), gather(1, "zx"))

    left_half = lax.broadcasted_iota(jnp.int32, (256, 128), 1) < 64

    def unpack(p, sq):
        w, x, z = lax.div(p, 8), lax.rem(lax.div(p, 2), 4), lax.rem(p, 2) * 2
        a = xb[w, x, z].astype(F32)
        b = xb[w, x, z + 1].astype(F32)
        top = jnp.where(left_half, a, pltpu.roll(b, 64, 1))
        low = jnp.where(left_half, pltpu.roll(a, 64, 1), b)
        at = pl.ds(pl.multiple_of(p * 128, 128), 128)
        xs[0:256, at] = top.astype(BF16)
        xs[256:512, at] = low.astype(BF16)
        return (sq[0] + top * top, sq[1] + low * low)

    zero = jnp.zeros((256, 128), F32)
    squares = lax.fori_loop(0, 16, unpack, (zero, zero))

    for b in range(2):
        mean_sq = jnp.sum(squares[b], axis=1, keepdims=True) * (1.0 / D)
        normed = (
            xs[256 * b : 256 * b + 256].astype(F32) * lax.rsqrt(mean_sq + 1e-06) * gin_ref[...]
        ).astype(BF16)
        hidden = jax.nn.gelu(
            jnp.dot(normed, win_ref[...], preferred_element_type=F32), approximate=True
        ).astype(BF16)
        for n in range(4):
            cols = slice(512 * n, 512 * n + 512)
            part[b, :, :, :, cols] = jnp.dot(
                hidden, wout_ref[:, cols], preferred_element_type=F32
            ).reshape(4, 4, 16, 512)

    def reduce(k, order, far1, near1, far2, near2):
        base = 1024 * k
        low, high = pl.ds(base, 512), pl.ds(base + 512, 512)
        stage = {base: pl.ds(0, 512), base + 512: pl.ds(512, 512)}
        first, second = order
        for dim, far, near, sel, count in (
            (first, far1, near1, {"w": None, second: None}, 8),
            (second, far2, near2, {"w": None, first: me[first]}, 2),
        ):
            def view(i, c, dim=dim, sel=sel):
                return part.at[(*ffn_lead({**sel, dim: i}), ALL, c)]

            lead = (ALL,) * (2 if count == 8 else 1)

            def far_at(n, far=far, lead=lead):
                return lambda c: far.at[(n, *lead)]

            def near_at(n, near=near, lead=lead):
                return lambda c: near.at[(n, *lead, ALL, stage[c.start])]

            def add(i, c, sources, dim=dim, sel=sel, count=count, far=far, near=near):
                def one(t, _):
                    w = lax.rem(t, 2)
                    q = lax.div(t, 2)
                    at = {"w": w, dim: i}
                    other = second if dim == first else first
                    at[other] = q if count == 8 else sel[other]
                    here = (at["w"], at["x"], at["z"], ALL, c)
                    got = (w, q) if count == 8 else (w,)
                    total = part[here]
                    for src in sources:
                        total = total + src(got, c)
                    part[here] = total
                    return 0

                lax.fori_loop(0, count, one, 0)

            def far_val(n, far=far):
                return lambda got, c: far[(n, *got)]

            def near_val(n, near=near):
                return lambda got, c: near[(n, *got, ALL, stage[c.start])]

            class Buffer:
                def __init__(self, ref_at, value):
                    self.ref_at, self.value = ref_at, value

                def __call__(self, *a):
                    return self.ref_at(*a) if len(a) == 1 else self.value(*a)

            yield from ring_reduce(
                links, me, dim, view,
                [Buffer(near_at(n), near_val(n)) for n in range(2)],
                [Buffer(far_at(n), far_val(n)) for n in range(2)],
                low, high, add,
            )
        cols = pl.ds(base, 1024)
        other = 1 - me_w
        got = links.send(
            part.at[other, me["x"], me["z"], :, cols], wrecv.at[:, cols], opposite
        )
        yield
        got.wait_recv()

    run(reduce(0, "zx", far_a, near_a, far_b, near_b), reduce(1, "xz", far_c, near_c, far_d, near_d))

    h = lax.axis_index("hidden")
    inputs = xs[pl.ds(pl.multiple_of(h * 16, 16), 16), :].astype(F32)
    encoded = inputs + (part[me_w, me["x"], me["z"]] + wrecv[...])
    mean_sq = jnp.mean(encoded * encoded, axis=1, keepdims=True)
    lat_ref[...] = (encoded * lax.rsqrt(mean_sq + 1e-06) * gout_ref[...]).astype(BF16)
    links.drain()


def feed_forward(packed, in_gain, w_in, w_out, out_gain):
    vmem = pl.BlockSpec(memory_space=pltpu.VMEM)
    copies = 2 * (1 + 2 * 6) + 2 * (2 * 6 + 1)
    return pl.pallas_call(
        ffn_kernel,
        out_shape=jax.ShapeDtypeStruct((16, D), BF16),
        in_specs=[vmem] * 5,
        out_specs=vmem,
        scratch_shapes=[
            pltpu.VMEM((2, 4, 4, 256, 128), BF16),
            pltpu.VMEM((512, D), BF16),
            pltpu.VMEM((2, 4, 4, 16, D), F32),
        ]
        + [
            pltpu.VMEM((2, *lead, 16, width), F32)
            for _ in range(2)
            for lead in ((2, 4), (2,))
            for width in (512, 1024)
        ]
        + [
            pltpu.VMEM((16, D), F32),
            pltpu.SemaphoreType.DMA((copies,)),
            pltpu.SemaphoreType.DMA((copies,)),
        ],
        compiler_params=pltpu.CompilerParams(
            collective_id=0, has_side_effects=True, vmem_limit_bytes=40 * 2**20
        ),
    )(packed, in_gain, w_in, w_out, out_gain)


ORDERS = ("xyz", "yzx", "zxy")
LAT_COLS = ((0, 384, 384), (768, 384, 256), (1408, 384, 256))
SUM_COLS = ((0, 256, 128), (384, 256, 128), (768, 128, 128))


def lead(sel):
    y = (ALL, ALL) if sel["y"] is None else (lax.rem(sel["y"], 2), lax.div(sel["y"], 2))
    return (*y, *(ALL if sel[d] is None else sel[d] for d in ("x", "z")))


def lead_sizes(dims):
    return tuple(s for d in ("y", "x", "z") if d in dims for s in ((2, 2) if d == "y" else (4,)))


def vocab_kernel(
    lat_ref, table_ref, tail_ref, out_ref, log_ref,
    lat, table, table_t, weights, scores, mixed, sums, stats, factors, got_stats,
    *rest,
):
    *stages, fin, ssem, rsem, load_sem = rest
    me = coords()
    y_lo, y_hi = lax.rem(me["y"], 2), lax.div(me["y"], 2)
    load = pltpu.make_async_copy(
        table_ref.at[pl.ds(0, 1184)], table.at[0, pl.ds(0, 1184)], load_sem
    )
    load.start()
    other_core = device({**me, "c": 1 - me["c"]})
    greet(
        [moved(me, d, s) for d in ("x", "y", "z") for s in (1, -1, 2)] + [other_core]
    )
    links = Links(ssem, rsem)
    lat[y_lo, y_hi, me["x"], me["z"]] = lat_ref[...]

    def gather(order, cols):
        start, n_low, n_high = cols
        low, high = pl.ds(start, n_low), pl.ds(start + n_low, n_high)
        sel = {d: me[d] for d in "xyz"}
        for dim in order:
            def view(i, c, dim=dim, sel=dict(sel)):
                return lat.at[(*lead({**sel, dim: i}), ALL, c)]
            yield from ring_gather(links, me, dim, view, low, high)
            sel[dim] = None

    def swap_table():
        yield
        table[0, 1184:HALF] = tail_ref[...]
        load.wait()
        swap = links.send(table.at[0], table.at[1], other_core)
        for j in range(19):
            if j % 4 == 1:
                yield
            if j == 9:
                swap.wait_recv()
            first = 128 * j
            if first + 128 <= HALF:
                block = table[0, first : first + 128]
            elif first >= HALF:
                block = table[1, first - HALF : first - HALF + 128]
            else:
                block = jnp.concatenate(
                    [table[0, first:HALF], table[1, 0 : first + 128 - HALF]], axis=0
                )
            table_t[:, first : first + 128] = block.T

    run(*(gather(o, c) for o, c in zip(ORDERS, LAT_COLS)), swap_table())

    scale = 5.0 / math.sqrt(D)
    row_id = lax.broadcasted_iota(jnp.int32, (VT, 256), 0)

    def score_block(b, _):
        frames = lat[lax.div(b, 2), lax.rem(b, 2)].reshape(256, D)

        def score_tile(t, top):
            half, lower = lax.div(t, 2), lax.rem(t, 2)
            rows = table[half, pl.ds(pl.multiple_of(lower * VT, VT), VT)]
            s = (
                lax.dot_general(
                    rows, frames, (((1,), (1,)), ((), ())), preferred_element_type=F32
                )
                * scale
            )
            s = jnp.where(row_id < ROWS - lower * VT, s, -1e30)
            scores[t] = s
            return jnp.maximum(top, jnp.max(s, axis=0, keepdims=True))

        top = lax.fori_loop(0, 4, score_tile, jnp.full((1, 256), -1e30, F32))
        lanes = pl.ds(pl.multiple_of(b * 256, 256), 256)

        def weigh(t, total):
            e = jnp.exp(scores[t] - top)
            weights[b, pl.ds(pl.multiple_of(t * VT, VT), VT)] = e.astype(BF16)
            return total + jnp.sum(e, axis=0, keepdims=True)

        total = lax.fori_loop(0, 4, weigh, jnp.zeros((1, 256), F32))
        stats[0, 0:1, lanes] = top
        stats[0, 1:2, lanes] = total
        return 0

    lax.fori_loop(0, 4, score_block, 0)

    def mix(b):
        def tile(n, _):
            rows = pl.ds(pl.multiple_of(n * 512, 512), 512)
            mixed[rows, 256 * b : 256 * b + 256] = jnp.dot(
                table_t[rows, :], weights[b], preferred_element_type=F32
            )
            return 0

        lax.fori_loop(0, 4, tile, 0)

    for phase, dim in enumerate("xyz"):
        copies = [
            links.send(stats.at[phase], got_stats.at[3 * phase + n], moved(me, dim, s))
            for n, s in enumerate((1, -1, 2))
        ]
        mix(phase)
        for copy in copies:
            copy.wait_recv()
        pairs = [stats[phase]] + [got_stats[3 * phase + n] for n in range(3)]
        top = functools.reduce(jnp.maximum, [p[0:1] for p in pairs])
        stats[phase + 1, 0:1] = top
        stats[phase + 1, 1:2] = sum(p[1:2] * jnp.exp(p[0:1] - top) for p in pairs)
    mix(3)

    factors[...] = jnp.exp(stats[0, 0:1] - stats[3, 0:1])

    def rescale(h, _):
        for yl in range(2):
            factor = factors[:, 512 * yl : 512 * yl + 512]
            for j in range(2):
                rows = pl.ds(pl.multiple_of(h * 64 + 32 * j, 32), 32)
                sums[yl, lax.div(h, 16), lax.rem(lax.div(h, 4), 4), lax.rem(h, 4), :, 512 * j : 512 * j + 512] = (
                    mixed[rows, 512 * yl : 512 * yl + 512] * factor
                ).astype(BF16)
        return 0

    lax.fori_loop(0, 32, rescale, 0)

    def reduce(k, order, cols):
        start, n_low, n_high = cols
        low, high = pl.ds(start, n_low), pl.ds(start + n_low, n_high)
        kept = set(order)
        sel = {d: None for d in order}
        for phase, dim in enumerate(order):
            kept = kept - {dim}
            sizes = lead_sizes(kept)
            far_low, far_high, near = stages[(k * 3 + phase) * 3 : (k * 3 + phase) * 3 + 3]
            count = math.prod(sizes)
            all_lead = (ALL,) * len(sizes)

            def inner(c, start=start):
                return pl.ds(c.start - start, c.size)

            def view(i, c, dim=dim, sel=dict(sel)):
                return sums.at[(*lead({**sel, dim: i}), ALL, c)]

            class Buffer:
                def __init__(self, ref, n, cut):
                    self.ref, self.n, self.cut = ref, n, cut

                def __call__(self, c, got=all_lead):
                    at = (*self.n, *got)
                    return self.ref.at[(*at, ALL, inner(c))] if self.cut else self.ref.at[at] if at else self.ref

                def value(self, c, got):
                    at = (*self.n, *got)
                    return self.ref[(*at, ALL, inner(c))] if self.cut else self.ref[(*at, ALL, ALL)]

            def add(i, c, sources, dim=dim, sel=dict(sel), kept=kept, sizes=sizes, count=count):
                def one(t, _):
                    got, rest_t = [], t
                    for s in reversed(sizes):
                        got.insert(0, lax.rem(rest_t, s))
                        rest_t = lax.div(rest_t, s)
                    got = tuple(got)
                    at = {**sel, dim: i}
                    left = list(got)
                    here = []
                    for d in ("y", "x", "z"):
                        n = 2 if d == "y" else 1
                        if d in kept:
                            here += left[:n]
                            left = left[n:]
                        elif d == "y":
                            here += [lax.rem(at["y"], 2), lax.div(at["y"], 2)]
                        else:
                            here.append(at[d])
                    here = (*here, ALL, c)
                    total = sums[here].astype(F32)
                    for src in sources:
                        total = total + src.value(c, got).astype(F32)
                    if kept or len(sources) == 1:
                        sums[here] = total.astype(BF16)
                    else:
                        fin[:, c] = total
                    return 0

                if count == 1:
                    one(0, 0)
                else:
                    lax.fori_loop(0, count, one, 0)

            yield from ring_reduce(
                links, me, dim, view,
                [Buffer(near, (0,), True), Buffer(near, (1,), True)],
                [Buffer(far_low, (), False), Buffer(far_high, (), False)],
                low, high, add,
            )
            sel[dim] = me[dim]

    run(*(reduce(k, o, c) for k, (o, c) in enumerate(zip(ORDERS, SUM_COLS))))

    lanes = pl.ds(pl.multiple_of(y_lo * 512, 512), 512)
    top, total = stats[3, 0:1, lanes], stats[3, 1:2, lanes]
    for j in range(2):
        out_ref[32 * j : 32 * j + 32, :] = (fin[:, 512 * j : 512 * j + 512] / total).astype(BF16)
    log_ref[...] = top + jnp.log(total)
    links.drain()


def vocabulary(latent, table, tail):
    vmem = pl.BlockSpec(memory_space=pltpu.VMEM)
    copies = 3 * 3 * 6 * 2 + 9 + 1
    stages = []
    for order, (start, n_low, n_high) in zip(ORDERS, SUM_COLS):
        for phase in range(3):
            sizes = lead_sizes(order[phase + 1 :])
            stages += [
                pltpu.VMEM((*sizes, 32, n_low), BF16),
                pltpu.VMEM((*sizes, 32, n_high), BF16),
                pltpu.VMEM((2, *sizes, 32, n_low + n_high), BF16),
            ]
    return pl.pallas_call(
        vocab_kernel,
        out_shape=(
            jax.ShapeDtypeStruct((64, 512), BF16),
            jax.ShapeDtypeStruct((1, 512), F32),
        ),
        in_specs=[vmem, pl.BlockSpec(memory_space=pl.ANY), vmem],
        out_specs=(vmem, vmem),
        scratch_shapes=[
            pltpu.VMEM((2, 2, 4, 4, 16, D), BF16),
            pltpu.VMEM((2, HALF, D), BF16),
            pltpu.VMEM((D, VP), BF16),
            pltpu.VMEM((4, VP, 256), BF16),
            pltpu.VMEM((4, VT, 256), F32),
            pltpu.VMEM((D, 1024), F32),
            pltpu.VMEM((2, 2, 4, 4, 32, 1024), BF16),
            pltpu.VMEM((4, 8, 1024), F32),
            pltpu.VMEM((1, 1024), F32),
            pltpu.VMEM((9, 8, 1024), F32),
            *stages,
            pltpu.VMEM((32, 1024), F32),
            pltpu.SemaphoreType.DMA((copies,)),
            pltpu.SemaphoreType.DMA((copies,)),
            pltpu.SemaphoreType.DMA,
        ],
        compiler_params=pltpu.CompilerParams(
            collective_id=1, has_side_effects=True, vmem_limit_bytes=60 * 2**20
        ),
    )(latent, table, tail)


def shards(frames_in, in_gain, w_in, w_out, out_gain, table):
    packed = jnp.concatenate([frames_in[:256], frames_in[256:]], axis=1)
    tail = jnp.pad(table[1184:], ((0, HALF - ROWS), (0, 0)))
    latent = feed_forward(packed, in_gain[None], w_in, w_out, out_gain[None])
    mixed, log_total = vocabulary(latent, table, tail)
    return (mixed.T, log_total.reshape(512))


def solution(mesh):
    placed = (
        P("frames", "hidden"),
        P(),
        P(None, "hidden"),
        P("hidden", None),
        P(),
        P(("frames", "hidden"), None),
    )
    return jax.shard_map(
        shards,
        mesh=mesh,
        in_specs=placed,
        out_specs=(P("frames", "hidden"), P("frames")),
        check_vma=False,
    )
```

```python
import functools
import math

import jax
import jax.numpy as jnp
from jax import lax
from jax.experimental import pallas as pl
from jax.experimental.pallas import tpu as pltpu
from jax.sharding import PartitionSpec as P

MESH = pl.DeviceIdType.MESH
D = 2048
ROWS = 1187
TAIL = 1168
REST = 32
AGAIN = REST - (ROWS - TAIL)
WIDE = 1280
F32 = jnp.float32
BF16 = jnp.bfloat16
ALL = slice(None)


def coords():
    f = lax.axis_index("frames")
    h = lax.axis_index("hidden")
    return {
        "x": lax.rem(lax.div(h, 4), 4),
        "y": lax.div(h, 16) * 2 + lax.div(f, 2),
        "z": lax.rem(h, 4),
        "c": lax.rem(f, 2),
    }


def device(at):
    return (
        lax.rem(at["y"], 2) * 2 + at["c"],
        lax.div(at["y"], 2) * 16 + at["x"] * 4 + at["z"],
    )


def moved(me, dim, by):
    return device({**me, dim: lax.rem(me[dim] + by + 4, 4)})


class Links:
    def __init__(self, send_sems, recv_sems):
        self.send_sems, self.recv_sems = send_sems, recv_sems
        self.count, self.flying = 0, []

    def send(self, src, dst, to):
        copy = pltpu.make_async_remote_copy(
            src_ref=src,
            dst_ref=dst,
            send_sem=self.send_sems.at[self.count],
            recv_sem=self.recv_sems.at[self.count],
            device_id=to,
            device_id_type=MESH,
        )
        copy.start()
        self.count += 1
        self.flying.append(copy)
        return copy

    def drain(self):
        for copy in self.flying:
            copy.wait_send()
        self.flying = []


def run(*streams):
    streams = list(streams)
    while streams:
        for stream in list(streams):
            try:
                next(stream)
            except StopIteration:
                streams.remove(stream)


def gather_stream(links, me, buf, order, direct):
    for k, dim in enumerate(order):
        fixed = tuple(me[d] for d in reversed(order[k + 1 :]))
        i = me[dim]
        right, left = moved(me, dim, 1), moved(me, dim, -1)
        before, after = lax.rem(i + 3, 4), lax.rem(i + 1, 4)

        def go(j, part, to, fixed=fixed):
            cut = () if part is None else (slice(2 * part, 2 * part + 2),)
            block = buf.at[(*fixed, j, *cut)]
            return links.send(block, block, to)

        if direct[k]:
            copies = [go(i, None, to) for to in (moved(me, dim, 2), right, left)]
            yield
            for copy in copies:
                copy.wait_recv()
            continue
        r_low, l_high = go(i, 0, right), go(i, 1, left)
        r_high, l_low = go(i, 1, right), go(i, 0, left)
        yield
        r_low.wait_recv()
        r_far = go(before, 0, right)
        l_high.wait_recv()
        l_far = go(after, 1, left)
        yield
        for copy in (r_high, l_low, r_far, l_far):
            copy.wait_recv()


def add_stream(links, me, buf, stages, order, direct, result):
    for k, dim in enumerate(order):
        fixed = tuple(me[d] for d in order[:k])
        left_dims = len(order) - 1 - k
        i = me[dim]
        right, left = moved(me, dim, 1), moved(me, dim, -1)
        before, after, across = lax.rem(i + 3, 4), lax.rem(i + 1, 4), lax.rem(i + 2, 4)

        def view(j, part, fixed=fixed):
            cut = () if part is None else (slice(2 * part, 2 * part + 2),)
            return buf.at[(*fixed, j, *cut)]

        def add(j, at, sources, fixed=fixed, left_dims=left_dims):
            total = buf[(*fixed, j, *at)].astype(F32)
            for ref, lead in sources:
                total = total + ref[lead].astype(F32)
            if left_dims == 0:
                result(total)
            else:
                buf[(*fixed, j, *at)] = total.astype(buf.dtype)

        if direct[k]:
            (near,) = stages[k]
            copies = [
                links.send(view(j, None), near.at[n], to)
                for n, (j, to) in enumerate(
                    ((across, moved(me, dim, 2)), (after, right), (before, left))
                )
            ]
            yield
            for copy in copies:
                copy.wait_recv()
            add(i, () if left_dims else (ALL, ALL), [(near, (n,)) for n in range(3)])
            continue
        far, near = stages[k]
        r_far = links.send(view(across, 0), far.at[0], right)
        l_far = links.send(view(across, 1), far.at[1], left)
        r_high = links.send(view(after, 1), near.at[0, 2:4], right)
        l_low = links.send(view(before, 0), near.at[1, 0:2], left)
        yield
        r_far.wait_recv()
        for t in range(2):
            add(after, (t,), [(far, (0, t))])
        r_low = links.send(view(after, 0), near.at[0, 0:2], right)
        l_far.wait_recv()
        for t in range(2):
            add(before, (2 + t,), [(far, (1, t))])
        l_high = links.send(view(before, 1), near.at[1, 2:4], left)
        yield
        r_high.wait_recv()
        l_high.wait_recv()
        for t in (2, 3):
            add(i, (t,), [(near, (0, t)), (near, (1, t))])
        l_low.wait_recv()
        r_low.wait_recv()
        for t in (0, 1):
            add(i, (t,), [(near, (0, t)), (near, (1, t))])


def stage_shapes(direct, rows, width, dtype):
    shapes = []
    for k, straight in enumerate(direct):
        block = (4,) * (len(direct) - 1 - k)
        if not straight:
            shapes.append(pltpu.VMEM((2, 2, *block[1:], rows, width), dtype))
        shapes.append(pltpu.VMEM((3 if straight else 2, *block, rows, width), dtype))
    return shapes


def by_phase(direct, refs):
    refs = iter(refs)
    return [(next(refs),) if straight else (next(refs), next(refs)) for straight in direct]


def greet(peers):
    barrier = pltpu.get_barrier_semaphore()
    for peer in peers:
        pl.semaphore_signal(barrier, inc=1, device_id=peer, device_id_type=MESH)
    pl.semaphore_wait(barrier, len(peers))


FFN_ORDERS = ("xz", "zx")
FFN_GATHER, FFN_ADD = (True, True), (False, True)
GATHER, ADD = (True, True, False), (False, True, True)


def feed_forward(links, me, other_core, x_ref, gin_ref, gout_ref, w_hbm, loads, refs, beside):
    xp, xs, win, wout, *refs = refs
    gathered, partial = refs[0:2], refs[2:4]
    n = (len(refs) - 4) // 2
    stages = [by_phase(FFN_ADD, refs[4 + n * k : 4 + n * k + n]) for k in range(2)]
    y_lo, half = lax.rem(me["y"], 2), lax.div(me["y"], 2)
    opposite = moved(me, "y", 2)
    cross = moved(me, "y", 2 * y_lo - 1)
    beside_y = moved(me, "y", 1 - 2 * y_lo)
    mine = y_lo * 2 + me["c"]

    def exchange_weights():
        theirs = (1 - y_lo) * 2 + me["c"]
        jobs = []
        for ref, hbm, rows, n in ((win, w_hbm[0], 512, 256), (wout, w_hbm[1], 64, 32)):
            for at in range(0, rows, n):
                own = pl.ds(pl.multiple_of(mine * rows + at, n), n)
                next_to = pl.ds(pl.multiple_of(theirs * rows + at, n), n)
                jobs.append((ref, hbm, own, next_to))

        def start(job):
            ref, hbm, own, next_to = job
            return links.send(hbm.at[next_to], ref.at[1, next_to], cross)

        got = [start(job) for job in jobs]
        passed, last = [], []

        def hand_over(n):
            ref, _, _, next_to = jobs[n]
            passed[n].wait_recv()
            last.append(links.send(ref.at[1, next_to], ref.at[1, next_to], other_core))

        for n, (ref, _, own, _) in enumerate(jobs):
            yield
            got[n].wait_recv()
            passed.append(links.send(ref.at[1, own], ref.at[1, own], beside_y))
            last.append(links.send(ref.at[1, own], ref.at[1, own], other_core))
            if n >= 1:
                hand_over(n - 1)
        yield
        hand_over(len(jobs) - 1)
        yield
        for copy in last:
            copy.wait_recv()

    lanes = lax.broadcasted_iota(jnp.int32, (256, 128), 1) < 64

    def exchange_frames():
        xp[half] = jnp.concatenate([x_ref[:, 0:256], x_ref[:, 256:512]], axis=0).T
        got = links.send(xp.at[half], xp.at[half], opposite)
        yield
        got.wait_recv()
        p = [xp[0].astype(F32), xp[1].astype(F32)]
        r = [pltpu.roll(v, 64, 1) for v in p]
        first = half == 0
        block = jnp.where(
            lanes, jnp.where(first, p[0], r[0]), jnp.where(first, r[1], p[1])
        ).astype(BF16)
        for k, order in enumerate(FFN_ORDERS):
            gathered[k][me[order[1]], me[order[0]]] = block[128 * k : 128 * k + 128]
        streams = [gather_stream(links, me, gathered[k], o, FFN_GATHER) for k, o in enumerate(FFN_ORDERS)]
        while streams:
            for stream in list(streams):
                try:
                    next(stream)
                except StopIteration:
                    streams.remove(stream)
            if streams:
                yield

    run(
        exchange_frames(),
        exchange_weights(),
        *beside,
    )
    few = lax.broadcasted_iota(jnp.int32, (128, 128), 1) < 64

    def unpack(p, squares):
        x, z = lax.div(p, 2), lax.rem(p, 2) * 2
        at = pl.multiple_of(p * 128, 128)
        sums = []
        for k in range(2):
            ref = gathered[k]
            a, b = (ref[z, x], ref[z + 1, x]) if k == 0 else (ref[x, z], ref[x, z + 1])
            a, b = a.astype(F32), b.astype(F32)
            rows = slice(128 * k, 128 * k + 128)
            top = jnp.where(few, a, pltpu.roll(b, 64, 1))
            low = jnp.where(few, pltpu.roll(a, 64, 1), b)
            xs[rows, pl.ds(at, 128)] = top.astype(BF16)
            xs[rows, pl.ds(at + 1024, 128)] = low.astype(BF16)
            sums.append(squares[k] + a * a + b * b)
        return tuple(sums)

    squares = lax.fori_loop(0, 8, unpack, (jnp.zeros((128, 128), F32),) * 2)
    mean_sq = jnp.sum(jnp.concatenate(squares, axis=0), axis=1, keepdims=True) * (1.0 / D)
    normed = (xs[...].astype(F32) * lax.rsqrt(mean_sq + 1e-06) * gin_ref[...]).astype(BF16)
    for load in loads:
        load.wait()
    hidden = [
        jax.nn.gelu(
            jnp.dot(normed, win[w], preferred_element_type=F32), approximate=True
        ).astype(BF16)
        for w in range(2)
    ]
    for k, order in enumerate(FFN_ORDERS):
        for part in range(2):
            cols = slice(1024 * k + 512 * part, 1024 * k + 512 * part + 512)
            block = jnp.dot(hidden[0], wout[0, :, cols], preferred_element_type=F32) + jnp.dot(
                hidden[1], wout[1, :, cols], preferred_element_type=F32
            )
            for t in range(16):
                at = (t // 4, t % 4) if order == "xz" else (t % 4, t // 4)
                partial[k][(*at, ALL, slice(512 * part, 512 * part + 512))] = block[16 * t : 16 * t + 16]
    found = {}
    run(
        *(
            add_stream(
                links, me, partial[k], stages[k], order, FFN_ADD,
                lambda value, k=k: found.update({k: value}),
            )
            for k, order in enumerate(FFN_ORDERS)
        )
    )
    row = pl.ds(pl.multiple_of(16 * (4 * me["x"] + me["z"]), 16), 16)
    total = jnp.concatenate([found[0], found[1]], axis=1)
    encoded = xs[row, :].astype(F32) + total
    mean_sq = jnp.mean(encoded * encoded, axis=1, keepdims=True)
    return (encoded * lax.rsqrt(mean_sq + 1e-06) * gout_ref[...]).astype(BF16)


FFN_SCRATCH = (
    [
        pltpu.VMEM((2, 256, 128), BF16),
        pltpu.VMEM((256, D), BF16),
        pltpu.VMEM((2, D, 256), BF16),
        pltpu.VMEM((2, 256, D), BF16),
    ]
    + [pltpu.VMEM((4, 4, 128, 128), BF16)] * 2
    + [pltpu.VMEM((4, 4, 16, 1024), F32)] * 2
    + stage_shapes(FFN_ADD, 16, 1024, F32) * 2
)
FFN_COPIES = 1 + 2 * (3 + 3) + 4 * 4 + 2 * (6 + 3)


ORDERS = ("xyz", "yzx", "zxy")
SPLITS = ((0, 384), (384, 384), (768, 256))


def kernel(
    x_ref, gin_ref, gout_ref, win_hbm, wout_hbm, table_hbm, tail_ref, out_ref, log_ref,
    turned, pieces, lat, scores, weights, stats, got_stats, factors, fin,
    *rest,
):
    ffn_refs, rest = rest[: len(FFN_SCRATCH)], rest[len(FFN_SCRATCH) :]
    buffers = [rest[0:3], rest[3:6]]
    *stages, ssem, rsem, load_sem = rest[6:]
    me = coords()
    y_lo, y_hi = lax.rem(me["y"], 2), lax.div(me["y"], 2)
    load_in = pltpu.make_async_copy(win_hbm, ffn_refs[2].at[0], load_sem.at[0])
    load_out = pltpu.make_async_copy(wout_hbm, ffn_refs[3].at[0], load_sem.at[1])
    load_in.start()
    load_out.start()

    def load_piece(p):
        n = min(256, TAIL - 256 * p)
        copy = pltpu.make_async_copy(
            table_hbm.at[pl.ds(256 * p, n)], pieces.at[p % 2, pl.ds(0, n)], load_sem.at[2 + p]
        )
        copy.start()
        return copy

    coming = [load_piece(0), load_piece(1)]
    other_core = device({**me, "c": 1 - me["c"]})
    greet([moved(me, d, s) for d in ("x", "y", "z") for s in (1, -1, 2)] + [other_core])
    links = Links(ssem, rsem)
    swaps = []

    def turn_table():
        yield
        for p in range(5):
            coming[p].wait()
            if p == 4:
                pieces[0, TAIL - 1024 : TAIL + REST - 1024] = tail_ref[...]
                pieces[0, TAIL + REST - 1024 : 256] = jnp.zeros((WIDE - TAIL - REST, D), BF16)
            for q in range(2):
                block = pieces[p % 2, 128 * q : 128 * q + 128]
                at = 256 * p + 128 * q
                turned[0, :, at : at + 128] = block.T
            if p + 2 < 5:
                coming.append(load_piece(p + 2))
            if p < 4:
                yield
        swaps.append(links.send(turned.at[0], turned.at[1], other_core))

    latent = feed_forward(
        links, me, other_core, x_ref, gin_ref, gout_ref, (win_hbm, wout_hbm), (load_in, load_out),
        ffn_refs, (turn_table(),),
    )
    for s in range(2):
        for buf, order, (start, width) in zip(buffers[s], ORDERS, SPLITS):
            at = 1024 * s + start
            buf[tuple(me[d] for d in reversed(order))] = latent[:, at : at + width]

    done = set()

    def then(stream, *keys):
        yield from stream
        done.update(keys)

    def after(keys, stream):
        while not set(keys) <= done:
            yield
        yield from stream

    scale = 5.0 / math.sqrt(D)

    def collect(s):
        def block(t, _):
            at = {"y": lax.div(t, 16), "x": lax.rem(lax.div(t, 4), 4), "z": lax.rem(t, 4)}
            to = (lax.rem(at["y"], 2), lax.div(at["y"], 2), at["x"], at["z"])
            for buf, order, (start, width) in zip(buffers[s], ORDERS, SPLITS):
                cols = slice(1024 * s + start, 1024 * s + start + width)
                lat[(*to, ALL, cols)] = buf[tuple(at[d] for d in reversed(order))]
            return 0

        lax.fori_loop(0, 64, block, 0)

    def score(s, g):
        frames = lat[:, g, :, :, :, 1024 * s : 1024 * s + 1024].reshape(512, 1024)

        def tile(t, _):
            half, n = lax.div(t, 5), lax.rem(t, 5)
            cols = pl.ds(pl.multiple_of(n * 256, 256), 256)
            at = pl.ds(pl.multiple_of(t * 256, 256), 256)
            product = jnp.dot(
                frames, turned[half, 1024 * s : 1024 * s + 1024, cols], preferred_element_type=F32
            )
            scores[g, :, at] = product if s == 0 else scores[g, :, at] + product
            return 0

        lax.fori_loop(0, 10, tile, 0)

    lane_id = lax.broadcasted_iota(jnp.int32, (1, 2 * WIDE), 1)
    place = lax.rem(lane_id, WIDE)
    real = (place < TAIL) | ((place >= TAIL + AGAIN) & (place < TAIL + REST))

    def softmax(g):
        def rows(r, _):
            at = pl.ds(pl.multiple_of(r * 32, 32), 32)
            s = jnp.where(real, scores[g, at, :] * scale, -1e30)
            top = jnp.max(s, axis=1, keepdims=True)
            e = jnp.exp(s - top)
            weights[g, at, :] = e.astype(BF16)
            factors[0, at, :] = jnp.broadcast_to(top, (32, 128))
            factors[1, at, :] = jnp.broadcast_to(jnp.sum(e, axis=1, keepdims=True), (32, 128))
            return 0

        lax.fori_loop(0, 16, rows, 0)
        stats[g, 0, 0:1] = factors[0].T[0:1]
        stats[g, 0, 1:2] = factors[1].T[0:1]

    def share_stats(g):
        for phase, dim in enumerate("xyz"):
            copies = [
                links.send(stats.at[g, phase], got_stats.at[g, 3 * phase + n], moved(me, dim, s))
                for n, s in enumerate((1, -1, 2))
            ]
            yield
            for copy in copies:
                copy.wait_recv()
            pairs = [stats[g, phase]] + [got_stats[g, 3 * phase + n] for n in range(3)]
            top = functools.reduce(jnp.maximum, [p[0:1] for p in pairs])
            stats[g, phase + 1, 0:1] = top
            stats[g, phase + 1, 1:2] = sum(p[1:2] * jnp.exp(p[0:1] - top) for p in pairs)

    def mix(g, n):
        rows = slice(512 * n, 512 * n + 512)
        dims = (((1,), (1,)), ((), ()))

        def tile(q, _):
            frames = pl.ds(pl.multiple_of(q * 256, 256), 256)
            total = lax.dot_general(
                turned[0, rows, :], weights[g, frames, 0:WIDE], dims, preferred_element_type=F32
            ) + lax.dot_general(
                turned[1, rows, :], weights[g, frames, WIDE:], dims, preferred_element_type=F32
            )
            scores[g, :, pl.ds(pl.multiple_of(512 * n + q * 256, 256), 256)] = total
            return 0

        lax.fori_loop(0, 2, tile, 0)

    def rescale(g):
        factor = jnp.exp(stats[g, 0, 0:1] - stats[g, 3, 0:1])

        def block(h8, _):
            for n in range(4):
                h = 8 * n + h8
                y_up, x, z = lax.div(h, 16), lax.rem(lax.div(h, 4), 4), lax.rem(h, 4)
                for yl in range(2):
                    at = {"x": x, "y": 2 * y_up + yl, "z": z}
                    for buf, order, (start, width) in zip(buffers[g], ORDERS, SPLITS):
                        for c in range(width // 128):
                            unit = start // 128 + c
                            lane = 256 * yl + 128 * (unit % 2)
                            rows = pl.ds(pl.multiple_of(h8 * 64 + 16 * (unit // 2), 16), 16)
                            value = scores[g, rows, 512 * n + lane : 512 * n + lane + 128]
                            buf[(*(at[d] for d in order), ALL, slice(128 * c, 128 * c + 128))] = (
                                value * factor[:, lane : lane + 128]
                            ).astype(BF16)
            return 0

        lax.fori_loop(0, 8, block, 0)

    def wait_for(*keys):
        while not set(keys) <= done:
            yield

    def compute():
        yield from wait_for(*(f"lat0{k}" for k in range(3)))
        swaps[0].wait_recv()
        collect(0)
        for g in range(2):
            score(0, g)
            yield
        yield from wait_for(*(f"lat1{k}" for k in range(3)))
        collect(1)
        links.drain()
        for g in range(2):
            score(1, g)
            softmax(g)
            done.add(f"local{g}")
            yield
        for n in range(4):
            mix(0, n)
            if n % 2:
                yield
        yield from wait_for("stats0")
        rescale(0)
        done.add("sums0")
        yield
        for n in range(4):
            mix(1, n)
        yield from wait_for("stats1")
        rescale(1)
        done.add("sums1")

    def final():
        for g in range(2):
            yield from wait_for(*(f"out{g}{k}" for k in range(3)))
            lanes = pl.ds(pl.multiple_of(y_lo * 256, 256), 256)
            top, total = stats[g, 3, 0:1, lanes], stats[g, 3, 1:2, lanes]
            for j in range(4):
                out_ref[16 * j : 16 * j + 16, 256 * g : 256 * g + 256] = (
                    fin[g, :, 256 * j : 256 * j + 256] / total
                ).astype(BF16)
            log_ref[:, 256 * g : 256 * g + 256] = top + jnp.log(total)

    def delayed(stream, rounds):
        for _ in range(rounds):
            yield
        yield from stream

    streams = [
        then(delayed(gather_stream(links, me, buffers[s][k], o, GATHER), 2 * s), f"lat{s}{k}")
        for s in range(2)
        for k, o in enumerate(ORDERS)
    ]
    streams.append(compute())
    streams += [then(after([f"local{g}"], share_stats(g)), f"stats{g}") for g in range(2)]
    for g in range(2):
        for k, (o, (start, width)) in enumerate(zip(ORDERS, SPLITS)):
            def result(value, g=g, start=start, width=width):
                fin[g, :, start : start + width] = value

            n = len(stages) // 6
            at = n * (3 * g + k)
            stream = add_stream(
                links, me, buffers[g][k], by_phase(ADD, stages[at : at + n]), o, ADD, result
            )
            streams.append(then(after([f"sums{g}"], stream), f"out{g}{k}"))
    streams.append(final())
    run(*streams)
    links.drain()


def fused(frames_in, in_gain, out_gain, w_in, w_out, table, tail):
    vmem = pl.BlockSpec(memory_space=pltpu.VMEM)
    hbm = pl.BlockSpec(memory_space=pl.ANY)
    copies = FFN_COPIES + 1 + 2 * 9 + 2 * 3 * 2 * 12
    buffers, stages = [], []
    for _ in range(2):
        for _, width in SPLITS:
            buffers.append(pltpu.VMEM((4, 4, 4, 16, width), BF16))
            stages += stage_shapes(ADD, 16, width, BF16)
    return pl.pallas_call(
        kernel,
        out_shape=(
            jax.ShapeDtypeStruct((64, 512), BF16),
            jax.ShapeDtypeStruct((1, 512), F32),
        ),
        in_specs=[vmem] * 3 + [hbm] * 3 + [vmem],
        out_specs=(vmem, vmem),
        scratch_shapes=[
            pltpu.VMEM((2, D, WIDE), BF16),
            pltpu.VMEM((2, 256, D), BF16),
            pltpu.VMEM((2, 2, 4, 4, 16, D), BF16),
            pltpu.VMEM((2, 512, 2 * WIDE), F32),
            pltpu.VMEM((2, 512, 2 * WIDE), BF16),
            pltpu.VMEM((2, 4, 8, 512), F32),
            pltpu.VMEM((2, 9, 8, 512), F32),
            pltpu.VMEM((2, 512, 128), F32),
            pltpu.VMEM((2, 16, 1024), F32),
            *FFN_SCRATCH,
            *buffers,
            *stages,
            pltpu.SemaphoreType.DMA((copies,)),
            pltpu.SemaphoreType.DMA((copies,)),
            pltpu.SemaphoreType.DMA((7,)),
        ],
        compiler_params=pltpu.CompilerParams(
            collective_id=0, has_side_effects=True, vmem_limit_bytes=61 * 2**20
        ),
    )(frames_in, in_gain, out_gain, w_in, w_out, table, tail)


def shards(frames_in, in_gain, w_in, w_out, out_gain, table):
    tail = table[ROWS - REST :]
    mixed, log_total = fused(frames_in.T, in_gain[None], out_gain[None], w_in, w_out, table, tail)
    return (mixed.T, log_total.reshape(512))


def solution(mesh):
    placed = (
        P("frames", "hidden"),
        P(),
        P(None, "hidden"),
        P("hidden", None),
        P(),
        P(("frames", "hidden"), None),
    )
    return jax.shard_map(
        shards,
        mesh=mesh,
        in_specs=placed,
        out_specs=(P("frames", "hidden"), P("frames")),
        check_vma=False,
    )
```

```python
import functools
import math

import jax
import jax.numpy as jnp
from jax import lax
from jax.experimental import pallas as pl
from jax.experimental.pallas import tpu as pltpu
from jax.sharding import PartitionSpec as P

MESH = pl.DeviceIdType.MESH
D = 2048
ROWS = 1187
TAIL = 1168
REST = 32
AGAIN = REST - (ROWS - TAIL)
WIDE = 1280
F32 = jnp.float32
BF16 = jnp.bfloat16
ALL = slice(None)


def coords():
    f = lax.axis_index("frames")
    h = lax.axis_index("hidden")
    return {
        "x": lax.rem(lax.div(h, 4), 4),
        "y": lax.div(h, 16) * 2 + lax.div(f, 2),
        "z": lax.rem(h, 4),
        "c": lax.rem(f, 2),
    }


def device(at):
    return (
        lax.rem(at["y"], 2) * 2 + at["c"],
        lax.div(at["y"], 2) * 16 + at["x"] * 4 + at["z"],
    )


def moved(me, dim, by):
    return device({**me, dim: lax.rem(me[dim] + by + 4, 4)})


class Links:
    def __init__(self, send_sems, recv_sems):
        self.send_sems, self.recv_sems = send_sems, recv_sems
        self.count, self.flying = 0, []

    def send(self, src, dst, to):
        copy = pltpu.make_async_remote_copy(
            src_ref=src,
            dst_ref=dst,
            send_sem=self.send_sems.at[self.count],
            recv_sem=self.recv_sems.at[self.count],
            device_id=to,
            device_id_type=MESH,
        )
        copy.start()
        self.count += 1
        self.flying.append(copy)
        return copy

    def drain(self):
        for copy in self.flying:
            copy.wait_send()
        self.flying = []


def run(*streams):
    streams = list(streams)
    while streams:
        for stream in list(streams):
            try:
                next(stream)
            except StopIteration:
                streams.remove(stream)


def gather_stream(links, me, buf, order, direct):
    for k, dim in enumerate(order):
        fixed = tuple(me[d] for d in reversed(order[k + 1 :]))
        i = me[dim]
        right, left = moved(me, dim, 1), moved(me, dim, -1)
        before, after = lax.rem(i + 3, 4), lax.rem(i + 1, 4)

        def go(j, part, to, fixed=fixed):
            cut = () if part is None else (slice(2 * part, 2 * part + 2),)
            block = buf.at[(*fixed, j, *cut)]
            return links.send(block, block, to)

        if direct[k]:
            copies = [go(i, None, to) for to in (moved(me, dim, 2), right, left)]
            yield
            for copy in copies:
                copy.wait_recv()
            continue
        r_low, l_high = go(i, 0, right), go(i, 1, left)
        r_high, l_low = go(i, 1, right), go(i, 0, left)
        yield
        r_low.wait_recv()
        r_far = go(before, 0, right)
        l_high.wait_recv()
        l_far = go(after, 1, left)
        yield
        for copy in (r_high, l_low, r_far, l_far):
            copy.wait_recv()


def add_stream(links, me, buf, stages, order, direct, result):
    for k, dim in enumerate(order):
        fixed = tuple(me[d] for d in order[:k])
        left_dims = len(order) - 1 - k
        i = me[dim]
        right, left = moved(me, dim, 1), moved(me, dim, -1)
        before, after, across = lax.rem(i + 3, 4), lax.rem(i + 1, 4), lax.rem(i + 2, 4)

        def view(j, part, fixed=fixed):
            cut = () if part is None else (slice(2 * part, 2 * part + 2),)
            return buf.at[(*fixed, j, *cut)]

        def add(j, at, sources, fixed=fixed, left_dims=left_dims):
            total = buf[(*fixed, j, *at)].astype(F32)
            for ref, lead in sources:
                total = total + ref[lead].astype(F32)
            if left_dims == 0:
                result(total)
            else:
                buf[(*fixed, j, *at)] = total.astype(buf.dtype)

        if direct[k]:
            (near,) = stages[k]
            copies = [
                links.send(view(j, None), near.at[n], to)
                for n, (j, to) in enumerate(
                    ((across, moved(me, dim, 2)), (after, right), (before, left))
                )
            ]
            yield
            for copy in copies:
                copy.wait_recv()
            add(i, () if left_dims else (ALL, ALL), [(near, (n,)) for n in range(3)])
            continue
        far, near = stages[k]
        r_far = links.send(view(across, 0), far.at[0], right)
        l_far = links.send(view(across, 1), far.at[1], left)
        r_high = links.send(view(after, 1), near.at[0, 2:4], right)
        l_low = links.send(view(before, 0), near.at[1, 0:2], left)
        yield
        r_far.wait_recv()
        for t in range(2):
            add(after, (t,), [(far, (0, t))])
        r_low = links.send(view(after, 0), near.at[0, 0:2], right)
        l_far.wait_recv()
        for t in range(2):
            add(before, (2 + t,), [(far, (1, t))])
        l_high = links.send(view(before, 1), near.at[1, 2:4], left)
        yield
        r_high.wait_recv()
        l_high.wait_recv()
        for t in (2, 3):
            add(i, (t,), [(near, (0, t)), (near, (1, t))])
        l_low.wait_recv()
        r_low.wait_recv()
        for t in (0, 1):
            add(i, (t,), [(near, (0, t)), (near, (1, t))])


def stage_shapes(direct, rows, width, dtype):
    shapes = []
    for k, straight in enumerate(direct):
        block = (4,) * (len(direct) - 1 - k)
        if not straight:
            shapes.append(pltpu.VMEM((2, 2, *block[1:], rows, width), dtype))
        shapes.append(pltpu.VMEM((3 if straight else 2, *block, rows, width), dtype))
    return shapes


def by_phase(direct, refs):
    refs = iter(refs)
    return [(next(refs),) if straight else (next(refs), next(refs)) for straight in direct]


def greet(peers):
    barrier = pltpu.get_barrier_semaphore()
    for peer in peers:
        pl.semaphore_signal(barrier, inc=1, device_id=peer, device_id_type=MESH)
    pl.semaphore_wait(barrier, len(peers))


FFN_ORDERS = ("xz", "zx")
FFN_GATHER, FFN_ADD = (True, True), (False, True)
GATHER, ADD = (True, True, False), (False, True, True)


def feed_forward(links, me, other_core, x_ref, gin_ref, gout_ref, w_hbm, loads, refs, beside, beside_done):
    xp, xs, win, wout, *refs = refs
    gathered, partial = refs[0:2], refs[2:4]
    n = (len(refs) - 4) // 2
    stages = [by_phase(FFN_ADD, refs[4 + n * k : 4 + n * k + n]) for k in range(2)]
    done = beside_done
    y_lo, half = lax.rem(me["y"], 2), lax.div(me["y"], 2)
    opposite = moved(me, "y", 2)
    cross = moved(me, "y", 2 * y_lo - 1)
    beside_y = moved(me, "y", 1 - 2 * y_lo)
    mine = y_lo * 2 + me["c"]

    def exchange_weights():
        theirs = (1 - y_lo) * 2 + me["c"]
        jobs = []
        for ref, hbm, rows, n in ((win, w_hbm[0], 512, 256), (wout, w_hbm[1], 64, 32)):
            for at in range(0, rows, n):
                own = pl.ds(pl.multiple_of(mine * rows + at, n), n)
                next_to = pl.ds(pl.multiple_of(theirs * rows + at, n), n)
                jobs.append((ref, hbm, own, next_to))

        def start(job):
            ref, hbm, own, next_to = job
            return links.send(hbm.at[next_to], ref.at[1, next_to], cross)

        got = [start(job) for job in jobs]
        passed, last = [], []

        def hand_over(n):
            ref, _, _, next_to = jobs[n]
            passed[n].wait_recv()
            last.append(links.send(ref.at[1, next_to], ref.at[1, next_to], other_core))

        def settle(what, *which):
            for n in which:
                last[n].wait_recv()
            done.add(what)

        for n, (ref, _, own, _) in enumerate(jobs):
            yield
            got[n].wait_recv()
            passed.append(links.send(ref.at[1, own], ref.at[1, own], beside_y))
            last.append(links.send(ref.at[1, own], ref.at[1, own], other_core))
            if n >= 1:
                hand_over(n - 1)
            if n == 3:
                settle("w_in", 0, 1, 2, 4)
        yield
        hand_over(len(jobs) - 1)
        yield
        settle("w_out", 3, 5, 6, 7)

    lanes = lax.broadcasted_iota(jnp.int32, (256, 128), 1) < 64

    def exchange_frames():
        xp[half] = jnp.concatenate([x_ref[:, 0:256], x_ref[:, 256:512]], axis=0).T
        got = links.send(xp.at[half], xp.at[half], opposite)
        yield
        got.wait_recv()
        p = [xp[0].astype(F32), xp[1].astype(F32)]
        r = [pltpu.roll(v, 64, 1) for v in p]
        first = half == 0
        block = jnp.where(
            lanes, jnp.where(first, p[0], r[0]), jnp.where(first, r[1], p[1])
        ).astype(BF16)
        for k, order in enumerate(FFN_ORDERS):
            gathered[k][me[order[1]], me[order[0]]] = block[128 * k : 128 * k + 128]
        streams = [gather_stream(links, me, gathered[k], o, FFN_GATHER) for k, o in enumerate(FFN_ORDERS)]
        while streams:
            for stream in list(streams):
                try:
                    next(stream)
                except StopIteration:
                    streams.remove(stream)
            if streams:
                yield
        done.add("frames")

    def compute():
        while "frames" not in done:
            yield
        few = lax.broadcasted_iota(jnp.int32, (128, 128), 1) < 64

        def unpack(p, squares):
            x, z = lax.div(p, 2), lax.rem(p, 2) * 2
            at = pl.multiple_of(p * 128, 128)
            sums = []
            for k in range(2):
                ref = gathered[k]
                a, b = (ref[z, x], ref[z + 1, x]) if k == 0 else (ref[x, z], ref[x, z + 1])
                a, b = a.astype(F32), b.astype(F32)
                rows = slice(128 * k, 128 * k + 128)
                top = jnp.where(few, a, pltpu.roll(b, 64, 1))
                low = jnp.where(few, pltpu.roll(a, 64, 1), b)
                xs[rows, pl.ds(at, 128)] = top.astype(BF16)
                xs[rows, pl.ds(at + 1024, 128)] = low.astype(BF16)
                sums.append(squares[k] + a * a + b * b)
            return tuple(sums)

        squares = lax.fori_loop(0, 8, unpack, (jnp.zeros((128, 128), F32),) * 2)
        mean_sq = jnp.sum(jnp.concatenate(squares, axis=0), axis=1, keepdims=True) * (1.0 / D)
        normed = (xs[...].astype(F32) * lax.rsqrt(mean_sq + 1e-06) * gin_ref[...]).astype(BF16)
        while "w_in" not in done:
            yield
        for load in loads:
            load.wait()
        hidden = [
            jax.nn.gelu(
                jnp.dot(normed, win[w], preferred_element_type=F32), approximate=True
            ).astype(BF16)
            for w in range(2)
        ]
        while "w_out" not in done:
            yield
        for k, order in enumerate(FFN_ORDERS):
            for part in range(2):
                cols = slice(1024 * k + 512 * part, 1024 * k + 512 * part + 512)
                block = jnp.dot(hidden[0], wout[0, :, cols], preferred_element_type=F32) + jnp.dot(
                    hidden[1], wout[1, :, cols], preferred_element_type=F32
                )
                for t in range(16):
                    at = (t // 4, t % 4) if order == "xz" else (t % 4, t // 4)
                    partial[k][(*at, ALL, slice(512 * part, 512 * part + 512))] = block[16 * t : 16 * t + 16]

    run(exchange_frames(), exchange_weights(), *beside, compute())
    found = {}
    run(
        *(
            add_stream(
                links, me, partial[k], stages[k], order, FFN_ADD,
                lambda value, k=k: found.update({k: value}),
            )
            for k, order in enumerate(FFN_ORDERS)
        )
    )
    row = pl.ds(pl.multiple_of(16 * (4 * me["x"] + me["z"]), 16), 16)
    total = jnp.concatenate([found[0], found[1]], axis=1)
    encoded = xs[row, :].astype(F32) + total
    mean_sq = jnp.mean(encoded * encoded, axis=1, keepdims=True)
    return (encoded * lax.rsqrt(mean_sq + 1e-06) * gout_ref[...]).astype(BF16)


FFN_SCRATCH = (
    [
        pltpu.VMEM((2, 256, 128), BF16),
        pltpu.VMEM((256, D), BF16),
        pltpu.VMEM((2, D, 256), BF16),
        pltpu.VMEM((2, 256, D), BF16),
    ]
    + [pltpu.VMEM((4, 4, 128, 128), BF16)] * 2
    + [pltpu.VMEM((4, 4, 16, 1024), F32)] * 2
    + stage_shapes(FFN_ADD, 16, 1024, F32) * 2
)
FFN_COPIES = 1 + 2 * (3 + 3) + 4 * 4 + 2 * (6 + 3)


ORDERS = ("xyz", "yzx", "zxy")
SPLITS = ((0, 384), (384, 384), (768, 256))


def kernel(
    x_ref, gin_ref, gout_ref, win_hbm, wout_hbm, table_hbm, tail_ref, out_ref, log_ref,
    turned, pieces, lat, scores, weights, stats, got_stats, peaks, totals, fin,
    *rest,
):
    ffn_refs, rest = rest[: len(FFN_SCRATCH)], rest[len(FFN_SCRATCH) :]
    buffers = [rest[0:3], rest[3:6]]
    *stages, ssem, rsem, load_sem = rest[6:]
    me = coords()
    y_lo, y_hi = lax.rem(me["y"], 2), lax.div(me["y"], 2)
    load_in = pltpu.make_async_copy(win_hbm, ffn_refs[2].at[0], load_sem.at[0])
    load_out = pltpu.make_async_copy(wout_hbm, ffn_refs[3].at[0], load_sem.at[1])
    load_in.start()
    load_out.start()

    def load_piece(p):
        n = min(256, TAIL - 256 * p)
        copy = pltpu.make_async_copy(
            table_hbm.at[pl.ds(256 * p, n)], pieces.at[p % 2, pl.ds(0, n)], load_sem.at[2 + p]
        )
        copy.start()
        return copy

    coming = [load_piece(0), load_piece(1)]
    other_core = device({**me, "c": 1 - me["c"]})
    greet([moved(me, d, s) for d in ("x", "y", "z") for s in (1, -1, 2)] + [other_core])
    links = Links(ssem, rsem)
    swaps, weights_done = [], set()

    def turn_table():
        yield
        for p in range(5):
            coming[p].wait()
            if p == 4:
                pieces[0, TAIL - 1024 : TAIL + REST - 1024] = tail_ref[...]
                pieces[0, TAIL + REST - 1024 : 256] = jnp.zeros((WIDE - TAIL - REST, D), BF16)
            for q in range(2):
                block = pieces[p % 2, 128 * q : 128 * q + 128]
                at = 256 * p + 128 * q
                turned[0, :, at : at + 128] = block.T
            if p + 2 < 5:
                coming.append(load_piece(p + 2))
            if p < 4:
                yield
        while "w_out" not in weights_done:
            yield
        swaps.append(links.send(turned.at[0], turned.at[1], other_core))

    latent = feed_forward(
        links, me, other_core, x_ref, gin_ref, gout_ref, (win_hbm, wout_hbm), (load_in, load_out),
        ffn_refs, (turn_table(),), weights_done,
    )
    for s in range(2):
        for buf, order, (start, width) in zip(buffers[s], ORDERS, SPLITS):
            at = 1024 * s + start
            buf[tuple(me[d] for d in reversed(order))] = latent[:, at : at + width]

    done = set()

    def then(stream, *keys):
        yield from stream
        done.update(keys)

    def after(keys, stream):
        while not set(keys) <= done:
            yield
        yield from stream

    scale = 5.0 / math.sqrt(D) * math.log2(math.e)

    def collect(s):
        def block(t, _):
            at = {"y": lax.div(t, 16), "x": lax.rem(lax.div(t, 4), 4), "z": lax.rem(t, 4)}
            to = (lax.rem(at["y"], 2), lax.div(at["y"], 2), at["x"], at["z"])
            for buf, order, (start, width) in zip(buffers[s], ORDERS, SPLITS):
                cols = slice(1024 * s + start, 1024 * s + start + width)
                lat[(*to, ALL, cols)] = buf[tuple(at[d] for d in reversed(order))]
            return 0

        lax.fori_loop(0, 64, block, 0)

    tile_lane = lax.broadcasted_iota(jnp.int32, (1, 256), 1)

    def score_tile(s, g, t):
        frames = lat[:, g, :, :, :, 1024 * s : 1024 * s + 1024].reshape(512, 1024)
        half, n = lax.div(t, 5), lax.rem(t, 5)
        cols = pl.ds(pl.multiple_of(n * 256, 256), 256)
        at = pl.ds(pl.multiple_of(t * 256, 256), 256)
        product = jnp.dot(
            frames, turned[half, 1024 * s : 1024 * s + 1024, cols], preferred_element_type=F32
        )
        if s == 0:
            scores[g, :, at] = product
            return
        place = tile_lane + n * 256
        real = (place < TAIL) | ((place >= TAIL + AGAIN) & (place < TAIL + REST))
        value = jnp.where(real, (scores[g, :, at] + product) * scale, -1e30)
        scores[g, :, at] = value
        peaks[g] = jnp.maximum(peaks[g], jnp.maximum(value[:, :128], value[:, 128:]))

    def find_peaks(g):
        peaks[g] = jnp.broadcast_to(jnp.max(peaks[g], axis=1, keepdims=True), (512, 128))
        totals[g] = jnp.zeros((512, 128), F32)

    def weigh(g, rows, first, tiles):
        top = peaks[g, rows]
        total = totals[g, rows]
        for c in range(tiles):
            at = pl.ds(pl.multiple_of(first + 128 * c, 128), 128)
            e = jnp.exp2(scores[g, rows, at] - top)
            weights[g, rows, at] = e.astype(BF16)
            total = total + e
        totals[g, rows] = total

    def local_stats(g):
        stats[g, 0, 0:1] = peaks[g].T[0:1]
        total = jnp.broadcast_to(jnp.sum(totals[g], axis=1, keepdims=True), (512, 128))
        stats[g, 0, 1:2] = total.T[0:1]
        done.add(f"local{g}")

    def loop(first, last, *bodies):
        def step(t, _):
            for body in bodies:
                body(t)
            return 0

        lax.fori_loop(first, last, step, 0)

    def share_stats(g):
        for phase, dim in enumerate("xyz"):
            copies = [
                links.send(stats.at[g, phase], got_stats.at[g, 3 * phase + n], moved(me, dim, s))
                for n, s in enumerate((1, -1, 2))
            ]
            yield
            for copy in copies:
                copy.wait_recv()
            pairs = [stats[g, phase]] + [got_stats[g, 3 * phase + n] for n in range(3)]
            top = functools.reduce(jnp.maximum, [p[0:1] for p in pairs])
            stats[g, phase + 1, 0:1] = top
            stats[g, phase + 1, 1:2] = sum(p[1:2] * jnp.exp2(p[0:1] - top) for p in pairs)

    def mix_tile(g, t):
        n, q = lax.div(t, 2), lax.rem(t, 2)
        rows = pl.ds(pl.multiple_of(n * 512, 512), 512)
        frames = pl.ds(pl.multiple_of(q * 256, 256), 256)
        dims = (((1,), (1,)), ((), ()))
        scores[g, :, pl.ds(pl.multiple_of(t * 256, 256), 256)] = lax.dot_general(
            turned[0, rows, :], weights[g, frames, 0:WIDE], dims, preferred_element_type=F32
        ) + lax.dot_general(
            turned[1, rows, :], weights[g, frames, WIDE:], dims, preferred_element_type=F32
        )

    def rescale(g):
        factor = jnp.exp2(stats[g, 0, 0:1] - stats[g, 3, 0:1])

        def block(h8, _):
            for n in range(4):
                h = 8 * n + h8
                y_up, x, z = lax.div(h, 16), lax.rem(lax.div(h, 4), 4), lax.rem(h, 4)
                for yl in range(2):
                    at = {"x": x, "y": 2 * y_up + yl, "z": z}
                    for buf, order, (start, width) in zip(buffers[g], ORDERS, SPLITS):
                        for c in range(width // 128):
                            unit = start // 128 + c
                            lane = 256 * yl + 128 * (unit % 2)
                            rows = pl.ds(pl.multiple_of(h8 * 64 + 16 * (unit // 2), 16), 16)
                            value = scores[g, rows, 512 * n + lane : 512 * n + lane + 128]
                            buf[(*(at[d] for d in order), ALL, slice(128 * c, 128 * c + 128))] = (
                                value * factor[:, lane : lane + 128]
                            ).astype(BF16)
            return 0

        lax.fori_loop(0, 8, block, 0)

    def wait_for(*keys):
        while not set(keys) <= done:
            yield

    def compute():
        yield from wait_for(*(f"lat0{k}" for k in range(3)))
        swaps[0].wait_recv()
        collect(0)
        for g in range(2):
            loop(0, 10, functools.partial(score_tile, 0, g))
            peaks[g] = jnp.full((512, 128), -1e30, F32)
            yield
        yield from wait_for(*(f"lat1{k}" for k in range(3)))
        collect(1)
        links.drain()
        loop(0, 10, functools.partial(score_tile, 1, 0))
        find_peaks(0)
        loop(
            0, 10, functools.partial(score_tile, 1, 1), lambda t: weigh(0, ALL, t * 256, 2)
        )
        local_stats(0)
        yield
        find_peaks(1)
        for part in range(2):
            loop(
                4 * part, 4 * part + 4, functools.partial(mix_tile, 0),
                lambda t: weigh(1, pl.ds(pl.multiple_of(t * 64, 64), 64), 0, 20),
            )
            if part == 1:
                local_stats(1)
            yield
        yield from wait_for("stats0")
        rescale(0)
        done.add("sums0")
        yield
        for part in range(2):
            loop(4 * part, 4 * part + 4, functools.partial(mix_tile, 1))
            yield
        yield from wait_for("stats1")
        rescale(1)
        done.add("sums1")

    def final():
        for g in range(2):
            yield from wait_for(*(f"out{g}{k}" for k in range(3)))
            lanes = pl.ds(pl.multiple_of(y_lo * 256, 256), 256)
            top, total = stats[g, 3, 0:1, lanes], stats[g, 3, 1:2, lanes]
            for j in range(4):
                out_ref[16 * j : 16 * j + 16, 256 * g : 256 * g + 256] = (
                    fin[g, :, 256 * j : 256 * j + 256] / total
                ).astype(BF16)
            log_ref[:, 256 * g : 256 * g + 256] = top * math.log(2.0) + jnp.log(total)

    def delayed(stream, rounds):
        for _ in range(rounds):
            yield
        yield from stream

    streams = [
        then(delayed(gather_stream(links, me, buffers[s][k], o, GATHER), 2 * s), f"lat{s}{k}")
        for s in range(2)
        for k, o in enumerate(ORDERS)
    ]
    streams.append(compute())
    streams += [then(after([f"local{g}"], share_stats(g)), f"stats{g}") for g in range(2)]
    for g in range(2):
        for k, (o, (start, width)) in enumerate(zip(ORDERS, SPLITS)):
            def result(value, g=g, start=start, width=width):
                fin[g, :, start : start + width] = value

            n = len(stages) // 6
            at = n * (3 * g + k)
            stream = add_stream(
                links, me, buffers[g][k], by_phase(ADD, stages[at : at + n]), o, ADD, result
            )
            streams.append(then(after([f"sums{g}"], stream), f"out{g}{k}"))
    streams.append(final())
    run(*streams)
    links.drain()


def fused(frames_in, in_gain, out_gain, w_in, w_out, table, tail):
    vmem = pl.BlockSpec(memory_space=pltpu.VMEM)
    hbm = pl.BlockSpec(memory_space=pl.ANY)
    copies = FFN_COPIES + 1 + 2 * 9 + 2 * 3 * 2 * 12
    buffers, stages = [], []
    for _ in range(2):
        for _, width in SPLITS:
            buffers.append(pltpu.VMEM((4, 4, 4, 16, width), BF16))
            stages += stage_shapes(ADD, 16, width, BF16)
    return pl.pallas_call(
        kernel,
        out_shape=(
            jax.ShapeDtypeStruct((64, 512), BF16),
            jax.ShapeDtypeStruct((1, 512), F32),
        ),
        in_specs=[vmem] * 3 + [hbm] * 3 + [vmem],
        out_specs=(vmem, vmem),
        scratch_shapes=[
            pltpu.VMEM((2, D, WIDE), BF16),
            pltpu.VMEM((2, 256, D), BF16),
            pltpu.VMEM((2, 2, 4, 4, 16, D), BF16),
            pltpu.VMEM((2, 512, 2 * WIDE), F32),
            pltpu.VMEM((2, 512, 2 * WIDE), BF16),
            pltpu.VMEM((2, 4, 8, 512), F32),
            pltpu.VMEM((2, 9, 8, 512), F32),
            pltpu.VMEM((2, 512, 128), F32),
            pltpu.VMEM((2, 512, 128), F32),
            pltpu.VMEM((2, 16, 1024), F32),
            *FFN_SCRATCH,
            *buffers,
            *stages,
            pltpu.SemaphoreType.DMA((copies,)),
            pltpu.SemaphoreType.DMA((copies,)),
            pltpu.SemaphoreType.DMA((7,)),
        ],
        compiler_params=pltpu.CompilerParams(
            collective_id=0, has_side_effects=True, vmem_limit_bytes=61 * 2**20
        ),
    )(frames_in, in_gain, out_gain, w_in, w_out, table, tail)


def shards(frames_in, in_gain, w_in, w_out, out_gain, table):
    tail = table[ROWS - REST :]
    mixed, log_total = fused(frames_in.T, in_gain[None], out_gain[None], w_in, w_out, table, tail)
    return (mixed.T, log_total.reshape(512))


def solution(mesh):
    placed = (
        P("frames", "hidden"),
        P(),
        P(None, "hidden"),
        P("hidden", None),
        P(),
        P(("frames", "hidden"), None),
    )
    return jax.shard_map(
        shards,
        mesh=mesh,
        in_specs=placed,
        out_specs=(P("frames", "hidden"), P("frames")),
        check_vma=False,
    )
```

```python
import functools
import math

import jax
import jax.numpy as jnp
from jax import lax
from jax.experimental import pallas as pl
from jax.experimental.pallas import tpu as pltpu
from jax.sharding import PartitionSpec as P

MESH = pl.DeviceIdType.MESH
D = 2048
ROWS = 1187
TAIL = 1168
REST = 32
AGAIN = REST - (ROWS - TAIL)
WIDE = 1280
SCORE = 1280
F32 = jnp.float32
BF16 = jnp.bfloat16
ALL = slice(None)


def coords():
    f = lax.axis_index("frames")
    h = lax.axis_index("hidden")
    return {
        "x": lax.rem(lax.div(h, 4), 4),
        "y": lax.div(h, 16) * 2 + lax.div(f, 2),
        "z": lax.rem(h, 4),
        "c": lax.rem(f, 2),
    }


def device(at):
    return (
        lax.rem(at["y"], 2) * 2 + at["c"],
        lax.div(at["y"], 2) * 16 + at["x"] * 4 + at["z"],
    )


def moved(me, dim, by):
    return device({**me, dim: lax.rem(me[dim] + by + 4, 4)})


class Links:
    def __init__(self, send_sems, recv_sems):
        self.send_sems, self.recv_sems = send_sems, recv_sems
        self.count, self.flying = 0, []

    def send(self, src, dst, to):
        copy = pltpu.make_async_remote_copy(
            src_ref=src,
            dst_ref=dst,
            send_sem=self.send_sems.at[self.count],
            recv_sem=self.recv_sems.at[self.count],
            device_id=to,
            device_id_type=MESH,
        )
        copy.start()
        self.count += 1
        self.flying.append(copy)
        return copy

    def drain(self):
        for copy in self.flying:
            copy.wait_send()
        self.flying = []


def run(*streams):
    streams = list(streams)
    while streams:
        for stream in list(streams):
            try:
                next(stream)
            except StopIteration:
                streams.remove(stream)


def gather_stream(links, me, buf, order, direct):
    for k, dim in enumerate(order):
        fixed = tuple(me[d] for d in reversed(order[k + 1 :]))
        i = me[dim]
        right, left = moved(me, dim, 1), moved(me, dim, -1)
        before, after = lax.rem(i + 3, 4), lax.rem(i + 1, 4)

        def go(j, part, to, fixed=fixed):
            cut = () if part is None else (slice(2 * part, 2 * part + 2),)
            block = buf.at[(*fixed, j, *cut)]
            return links.send(block, block, to)

        if direct[k]:
            copies = [go(i, None, to) for to in (moved(me, dim, 2), right, left)]
            yield
            for copy in copies:
                copy.wait_recv()
            continue
        r_low, l_high = go(i, 0, right), go(i, 1, left)
        r_high, l_low = go(i, 1, right), go(i, 0, left)
        yield
        r_low.wait_recv()
        r_far = go(before, 0, right)
        l_high.wait_recv()
        l_far = go(after, 1, left)
        yield
        for copy in (r_high, l_low, r_far, l_far):
            copy.wait_recv()


def add_stream(links, me, buf, stages, order, direct, result):
    for k, dim in enumerate(order):
        fixed = tuple(me[d] for d in order[:k])
        left_dims = len(order) - 1 - k
        i = me[dim]
        right, left = moved(me, dim, 1), moved(me, dim, -1)
        before, after, across = lax.rem(i + 3, 4), lax.rem(i + 1, 4), lax.rem(i + 2, 4)

        def view(j, part, fixed=fixed):
            cut = () if part is None else (slice(2 * part, 2 * part + 2),)
            return buf.at[(*fixed, j, *cut)]

        def add(j, at, sources, fixed=fixed, left_dims=left_dims):
            total = buf[(*fixed, j, *at)].astype(F32)
            for ref, lead in sources:
                total = total + ref[lead].astype(F32)
            if left_dims == 0:
                result(total)
            else:
                buf[(*fixed, j, *at)] = total.astype(buf.dtype)

        if direct[k]:
            (near,) = stages[k]
            copies = [
                links.send(view(j, None), near.at[n], to)
                for n, (j, to) in enumerate(
                    ((across, moved(me, dim, 2)), (after, right), (before, left))
                )
            ]
            yield
            for copy in copies:
                copy.wait_recv()
            add(i, () if left_dims else (ALL, ALL), [(near, (n,)) for n in range(3)])
            continue
        far, near = stages[k]
        r_far = links.send(view(across, 0), far.at[0], right)
        l_far = links.send(view(across, 1), far.at[1], left)
        r_high = links.send(view(after, 1), near.at[0, 2:4], right)
        l_low = links.send(view(before, 0), near.at[1, 0:2], left)
        yield
        r_far.wait_recv()
        for t in range(2):
            add(after, (t,), [(far, (0, t))])
        r_low = links.send(view(after, 0), near.at[0, 0:2], right)
        l_far.wait_recv()
        for t in range(2):
            add(before, (2 + t,), [(far, (1, t))])
        l_high = links.send(view(before, 1), near.at[1, 2:4], left)
        yield
        r_high.wait_recv()
        l_high.wait_recv()
        for t in (2, 3):
            add(i, (t,), [(near, (0, t)), (near, (1, t))])
        l_low.wait_recv()
        r_low.wait_recv()
        for t in (0, 1):
            add(i, (t,), [(near, (0, t)), (near, (1, t))])


def stage_shapes(direct, rows, width, dtype):
    shapes = []
    for k, straight in enumerate(direct):
        block = (4,) * (len(direct) - 1 - k)
        if not straight:
            shapes.append(pltpu.VMEM((2, 2, *block[1:], rows, width), dtype))
        shapes.append(pltpu.VMEM((3 if straight else 2, *block, rows, width), dtype))
    return shapes


def by_phase(direct, refs):
    refs = iter(refs)
    return [(next(refs),) if straight else (next(refs), next(refs)) for straight in direct]


def greet(peers):
    barrier = pltpu.get_barrier_semaphore()
    for peer in peers:
        pl.semaphore_signal(barrier, inc=1, device_id=peer, device_id_type=MESH)
    pl.semaphore_wait(barrier, len(peers))


FFN_ORDERS = ("xz", "zx")
FFN_GATHER, FFN_ADD = (True, True), (False, True)
GATHER, ADD = (True, True, False), (False, True, True)


def feed_forward(links, me, other_core, x_ref, gin_ref, gout_ref, w_hbm, loads, refs, beside, beside_done):
    xp, xs, win, wout, *refs = refs
    gathered, partial = refs[0:2], refs[2:4]
    n = (len(refs) - 4) // 2
    stages = [by_phase(FFN_ADD, refs[4 + n * k : 4 + n * k + n]) for k in range(2)]
    done = beside_done
    y_lo, half = lax.rem(me["y"], 2), lax.div(me["y"], 2)
    opposite = moved(me, "y", 2)
    cross = moved(me, "y", 2 * y_lo - 1)
    beside_y = moved(me, "y", 1 - 2 * y_lo)
    mine = y_lo * 2 + me["c"]

    def exchange_weights():
        theirs = (1 - y_lo) * 2 + me["c"]
        jobs = []
        for ref, hbm, rows, n in ((win, w_hbm[0], 512, 256), (wout, w_hbm[1], 64, 32)):
            for at in range(0, rows, n):
                own = pl.ds(pl.multiple_of(mine * rows + at, n), n)
                next_to = pl.ds(pl.multiple_of(theirs * rows + at, n), n)
                jobs.append((ref, hbm, own, next_to))

        def start(job):
            ref, hbm, own, next_to = job
            return links.send(hbm.at[next_to], ref.at[1, next_to], cross)

        got = [start(job) for job in jobs]
        passed, last = [], []

        def hand_over(n):
            ref, _, _, next_to = jobs[n]
            passed[n].wait_recv()
            last.append(links.send(ref.at[1, next_to], ref.at[1, next_to], other_core))

        def settle(what, *which):
            for n in which:
                last[n].wait_recv()
            done.add(what)

        for n, (ref, _, own, _) in enumerate(jobs):
            yield
            got[n].wait_recv()
            passed.append(links.send(ref.at[1, own], ref.at[1, own], beside_y))
            last.append(links.send(ref.at[1, own], ref.at[1, own], other_core))
            if n >= 1:
                hand_over(n - 1)
            if n == 3:
                settle("w_in", 0, 1, 2, 4)
        yield
        hand_over(len(jobs) - 1)
        yield
        settle("w_out", 3, 5, 6, 7)

    lanes = lax.broadcasted_iota(jnp.int32, (256, 128), 1) < 64

    def exchange_frames():
        xp[half] = jnp.concatenate([x_ref[:, 0:256], x_ref[:, 256:512]], axis=0).T
        got = links.send(xp.at[half], xp.at[half], opposite)
        yield
        got.wait_recv()
        p = [xp[0].astype(F32), xp[1].astype(F32)]
        r = [pltpu.roll(v, 64, 1) for v in p]
        first = half == 0
        block = jnp.where(
            lanes, jnp.where(first, p[0], r[0]), jnp.where(first, r[1], p[1])
        ).astype(BF16)
        for k, order in enumerate(FFN_ORDERS):
            gathered[k][me[order[1]], me[order[0]]] = block[128 * k : 128 * k + 128]
        streams = [gather_stream(links, me, gathered[k], o, FFN_GATHER) for k, o in enumerate(FFN_ORDERS)]
        while streams:
            for stream in list(streams):
                try:
                    next(stream)
                except StopIteration:
                    streams.remove(stream)
            if streams:
                yield
        done.add("frames")

    def compute():
        while "frames" not in done:
            yield
        few = lax.broadcasted_iota(jnp.int32, (128, 128), 1) < 64

        def unpack(p, squares):
            x, z = lax.div(p, 2), lax.rem(p, 2) * 2
            at = pl.multiple_of(p * 128, 128)
            sums = []
            for k in range(2):
                ref = gathered[k]
                a, b = (ref[z, x], ref[z + 1, x]) if k == 0 else (ref[x, z], ref[x, z + 1])
                a, b = a.astype(F32), b.astype(F32)
                rows = slice(128 * k, 128 * k + 128)
                top = jnp.where(few, a, pltpu.roll(b, 64, 1))
                low = jnp.where(few, pltpu.roll(a, 64, 1), b)
                xs[rows, pl.ds(at, 128)] = top.astype(BF16)
                xs[rows, pl.ds(at + 1024, 128)] = low.astype(BF16)
                sums.append(squares[k] + a * a + b * b)
            return tuple(sums)

        squares = lax.fori_loop(0, 8, unpack, (jnp.zeros((128, 128), F32),) * 2)
        mean_sq = jnp.sum(jnp.concatenate(squares, axis=0), axis=1, keepdims=True) * (1.0 / D)
        normed = (xs[...].astype(F32) * lax.rsqrt(mean_sq + 1e-06) * gin_ref[...]).astype(BF16)
        while "w_in" not in done:
            yield
        for load in loads:
            load.wait()
        hidden = [
            jax.nn.gelu(
                jnp.dot(normed, win[w], preferred_element_type=F32), approximate=True
            ).astype(BF16)
            for w in range(2)
        ]
        while "w_out" not in done:
            yield
        for k, order in enumerate(FFN_ORDERS):
            for part in range(2):
                cols = slice(1024 * k + 512 * part, 1024 * k + 512 * part + 512)
                block = jnp.dot(hidden[0], wout[0, :, cols], preferred_element_type=F32) + jnp.dot(
                    hidden[1], wout[1, :, cols], preferred_element_type=F32
                )
                for t in range(16):
                    at = (t // 4, t % 4) if order == "xz" else (t % 4, t // 4)
                    partial[k][(*at, ALL, slice(512 * part, 512 * part + 512))] = block[16 * t : 16 * t + 16]

    run(exchange_frames(), exchange_weights(), *beside, compute())
    found = {}
    run(
        *(
            add_stream(
                links, me, partial[k], stages[k], order, FFN_ADD,
                lambda value, k=k: found.update({k: value}),
            )
            for k, order in enumerate(FFN_ORDERS)
        )
    )
    row = pl.ds(pl.multiple_of(16 * (4 * me["x"] + me["z"]), 16), 16)
    total = jnp.concatenate([found[0], found[1]], axis=1)
    encoded = xs[row, :].astype(F32) + total
    mean_sq = jnp.mean(encoded * encoded, axis=1, keepdims=True)
    return (encoded * lax.rsqrt(mean_sq + 1e-06) * gout_ref[...]).astype(BF16)


FFN_SCRATCH = (
    [
        pltpu.VMEM((2, 256, 128), BF16),
        pltpu.VMEM((256, D), BF16),
        pltpu.VMEM((2, D, 256), BF16),
        pltpu.VMEM((2, 256, D), BF16),
    ]
    + [pltpu.VMEM((4, 4, 128, 128), BF16)] * 2
    + [pltpu.VMEM((4, 4, 16, 1024), F32)] * 2
    + stage_shapes(FFN_ADD, 16, 1024, F32) * 2
)
FFN_COPIES = 1 + 2 * (3 + 3) + 4 * 4 + 2 * (6 + 3)


ORDERS = ("xyz", "yzx", "zxy")
SPLITS = ((0, 384), (384, 384), (768, 256))


def kernel(
    x_ref, gin_ref, gout_ref, win_hbm, wout_hbm, table_hbm, tail_ref, out_ref, log_ref,
    turned, pieces, lat, scores, weights, stats, got_stats, sums, peaks, totals, fin,
    *rest,
):
    ffn_refs, rest = rest[: len(FFN_SCRATCH)], rest[len(FFN_SCRATCH) :]
    buffers = [rest[0:3], rest[3:6]]
    *stages, ssem, rsem, load_sem = rest[6:]
    me = coords()
    y_lo, y_hi = lax.rem(me["y"], 2), lax.div(me["y"], 2)
    load_in = pltpu.make_async_copy(win_hbm, ffn_refs[2].at[0], load_sem.at[0])
    load_out = pltpu.make_async_copy(wout_hbm, ffn_refs[3].at[0], load_sem.at[1])
    load_in.start()
    load_out.start()

    def load_piece(p):
        n = min(256, TAIL - 256 * p)
        copy = pltpu.make_async_copy(
            table_hbm.at[pl.ds(256 * p, n)], pieces.at[p % 2, pl.ds(0, n)], load_sem.at[2 + p]
        )
        copy.start()
        return copy

    coming = [load_piece(0), load_piece(1)]
    other_core = device({**me, "c": 1 - me["c"]})
    greet([moved(me, d, s) for d in ("x", "y", "z") for s in (1, -1, 2)] + [other_core])
    links = Links(ssem, rsem)
    swaps, weights_done = [], set()

    def turn_table():
        yield
        for p in range(5):
            coming[p].wait()
            if p == 4:
                pieces[0, TAIL - 1024 : TAIL + REST - 1024] = tail_ref[...]
                pieces[0, TAIL + REST - 1024 : 256] = jnp.zeros((WIDE - TAIL - REST, D), BF16)
            for q in range(2):
                block = pieces[p % 2, 128 * q : 128 * q + 128]
                at = 256 * p + 128 * q
                turned[0, :, at : at + 128] = block.T
            if p + 2 < 5:
                coming.append(load_piece(p + 2))
            if p < 4:
                yield
        while "w_out" not in weights_done:
            yield
        swaps.append(links.send(turned.at[0], turned.at[1], other_core))

    latent = feed_forward(
        links, me, other_core, x_ref, gin_ref, gout_ref, (win_hbm, wout_hbm), (load_in, load_out),
        ffn_refs, (turn_table(),), weights_done,
    )
    for s in range(2):
        for buf, order, (start, width) in zip(buffers[s], ORDERS, SPLITS):
            at = 1024 * s + start
            buf[tuple(me[d] for d in reversed(order))] = latent[:, at : at + width]

    done = set()

    def then(stream, *keys):
        yield from stream
        done.update(keys)

    def after(keys, stream):
        while not set(keys) <= done:
            yield
        yield from stream

    scale = 5.0 / math.sqrt(D) * math.log2(math.e)

    def collect():
        def block(t, _):
            at = {"y": lax.div(t, 16), "x": lax.rem(lax.div(t, 4), 4), "z": lax.rem(t, 4)}
            to = (lax.rem(at["y"], 2), lax.div(at["y"], 2), at["x"], at["z"])
            for s in range(2):
                for buf, order, (start, width) in zip(buffers[s], ORDERS, SPLITS):
                    cols = slice(1024 * s + start, 1024 * s + start + width)
                    lat[(*to, ALL, cols)] = buf[tuple(at[d] for d in reversed(order))]
            return 0

        lax.fori_loop(0, 64, block, 0)

    tile_lane = lax.broadcasted_iota(jnp.int32, (1, SCORE), 1)

    def score_tile(g, t):
        frames = lat[:, g].reshape(512, D)
        half, n = lax.div(t, WIDE // SCORE), lax.rem(t, WIDE // SCORE)
        cols = pl.ds(pl.multiple_of(n * SCORE, 128), SCORE)
        at = pl.ds(pl.multiple_of(t * SCORE, 128), SCORE)
        place = tile_lane + n * SCORE
        real = (place < TAIL) | ((place >= TAIL + AGAIN) & (place < TAIL + REST))
        product = jnp.dot(frames, turned[half, :, cols], preferred_element_type=F32)
        value = jnp.where(real, product * scale, -1e30)
        scores[g, :, at] = value
        peaks[g] = functools.reduce(
            jnp.maximum, [peaks[g]] + [value[:, c : c + 128] for c in range(0, SCORE, 128)]
        )

    def find_peaks(g):
        peaks[g] = jnp.broadcast_to(jnp.max(peaks[g], axis=1, keepdims=True), (512, 128))
        totals[g] = jnp.zeros((512, 128), F32)

    def weigh(g, rows, first, tiles):
        top = peaks[g, rows]
        total = totals[g, rows]
        for c in range(tiles):
            at = pl.ds(pl.multiple_of(first + 128 * c, 128), 128)
            e = jnp.exp2(scores[g, rows, at] - top)
            weights[g, rows, at] = e.astype(BF16)
            total = total + e
        totals[g, rows] = total

    def local_top(g):
        stats[0, g, 0, 0:1] = peaks[g].T[0:1]
        done.add(f"peak{g}")

    def local_sum(g):
        total = jnp.broadcast_to(jnp.sum(totals[g], axis=1, keepdims=True), (512, 128))
        sums[g] = total.T[0:1]

    def loop(first, last, *bodies):
        def step(t, _):
            for body in bodies:
                body(t)
            return 0

        lax.fori_loop(first, last, step, 0)

    def share(g, kind, combine):
        for phase, dim in enumerate("xyz"):
            copies = [
                links.send(
                    stats.at[kind, g, phase], got_stats.at[kind, g, 3 * phase + n], moved(me, dim, s)
                )
                for n, s in enumerate((1, -1, 2))
            ]
            yield
            for copy in copies:
                copy.wait_recv()
            parts = [stats[kind, g, phase]] + [got_stats[kind, g, 3 * phase + n] for n in range(3)]
            stats[kind, g, phase + 1] = functools.reduce(combine, parts)

    def share_sum(g):
        stats[1, g, 0, 0:1] = sums[g] * jnp.exp2(stats[0, g, 0, 0:1] - stats[0, g, 3, 0:1])
        yield from share(g, 1, jnp.add)

    def mix_tile(g, t):
        rows = pl.ds(pl.multiple_of(t * 512, 512), 512)
        dims = (((1,), (1,)), ((), ()))
        scores[g, :, pl.ds(pl.multiple_of(t * 512, 512), 512)] = lax.dot_general(
            turned[0, rows, :], weights[g, :, 0:WIDE], dims, preferred_element_type=F32
        ) + lax.dot_general(
            turned[1, rows, :], weights[g, :, WIDE:], dims, preferred_element_type=F32
        )

    def rescale(g):
        factor = jnp.exp2(stats[0, g, 0, 0:1] - stats[0, g, 3, 0:1])

        def block(h8, _):
            for n in range(4):
                h = 8 * n + h8
                y_up, x, z = lax.div(h, 16), lax.rem(lax.div(h, 4), 4), lax.rem(h, 4)
                for yl in range(2):
                    at = {"x": x, "y": 2 * y_up + yl, "z": z}
                    for buf, order, (start, width) in zip(buffers[g], ORDERS, SPLITS):
                        for c in range(width // 128):
                            unit = start // 128 + c
                            lane = 256 * yl + 128 * (unit % 2)
                            rows = pl.ds(pl.multiple_of(h8 * 64 + 16 * (unit // 2), 16), 16)
                            value = scores[g, rows, 512 * n + lane : 512 * n + lane + 128]
                            buf[(*(at[d] for d in order), ALL, slice(128 * c, 128 * c + 128))] = (
                                value * factor[:, lane : lane + 128]
                            ).astype(BF16)
            return 0

        lax.fori_loop(0, 8, block, 0)

    def wait_for(*keys):
        while not set(keys) <= done:
            yield

    def compute():
        yield from wait_for(*(f"lat{s}{k}" for s in range(2) for k in range(3)))
        swaps[0].wait_recv()
        collect()
        links.drain()
        peaks[...] = jnp.full((2, 512, 128), -1e30, F32)
        tiles = 2 * WIDE // SCORE
        loop(0, tiles, functools.partial(score_tile, 0))
        find_peaks(0)
        local_top(0)
        yield
        loop(
            0, tiles, functools.partial(score_tile, 1),
            lambda t: weigh(0, ALL, t * SCORE, SCORE // 128),
        )
        local_sum(0)
        find_peaks(1)
        local_top(1)
        yield
        for part in range(2):
            loop(
                2 * part, 2 * part + 2, functools.partial(mix_tile, 0),
                lambda t: weigh(1, pl.ds(pl.multiple_of(t * 128, 128), 128), 0, 20),
            )
            if part == 1:
                local_sum(1)
            yield
        yield from wait_for("stats0")
        rescale(0)
        done.add("sums0")
        yield
        for part in range(2):
            loop(2 * part, 2 * part + 2, functools.partial(mix_tile, 1))
            yield
        yield from wait_for("stats1")
        rescale(1)
        done.add("sums1")

    def final():
        for g in range(2):
            yield from wait_for(f"total{g}", *(f"out{g}{k}" for k in range(3)))
            lanes = pl.ds(pl.multiple_of(y_lo * 256, 256), 256)
            top, total = stats[0, g, 3, 0:1, lanes], stats[1, g, 3, 0:1, lanes]
            for j in range(4):
                out_ref[16 * j : 16 * j + 16, 256 * g : 256 * g + 256] = (
                    fin[g, :, 256 * j : 256 * j + 256] / total
                ).astype(BF16)
            log_ref[:, 256 * g : 256 * g + 256] = top * math.log(2.0) + jnp.log(total)

    streams = [
        then(gather_stream(links, me, buffers[s][k], o, GATHER), f"lat{s}{k}")
        for s in range(2)
        for k, o in enumerate(ORDERS)
    ]
    streams.append(compute())
    for g in range(2):
        streams.append(then(after([f"peak{g}"], share(g, 0, jnp.maximum)), f"stats{g}"))
        streams.append(then(after([f"sums{g}"], share_sum(g)), f"total{g}"))
    for g in range(2):
        for k, (o, (start, width)) in enumerate(zip(ORDERS, SPLITS)):
            def result(value, g=g, start=start, width=width):
                fin[g, :, start : start + width] = value

            n = len(stages) // 6
            at = n * (3 * g + k)
            stream = add_stream(
                links, me, buffers[g][k], by_phase(ADD, stages[at : at + n]), o, ADD, result
            )
            streams.append(then(after([f"sums{g}"], stream), f"out{g}{k}"))
    streams.append(final())
    run(*streams)
    links.drain()


def fused(frames_in, in_gain, out_gain, w_in, w_out, table, tail):
    vmem = pl.BlockSpec(memory_space=pltpu.VMEM)
    hbm = pl.BlockSpec(memory_space=pl.ANY)
    copies = FFN_COPIES + 1 + 2 * 18 + 2 * 3 * 2 * 12
    buffers, stages = [], []
    for _ in range(2):
        for _, width in SPLITS:
            buffers.append(pltpu.VMEM((4, 4, 4, 16, width), BF16))
            stages += stage_shapes(ADD, 16, width, BF16)
    return pl.pallas_call(
        kernel,
        out_shape=(
            jax.ShapeDtypeStruct((64, 512), BF16),
            jax.ShapeDtypeStruct((1, 512), F32),
        ),
        in_specs=[vmem] * 3 + [hbm] * 3 + [vmem],
        out_specs=(vmem, vmem),
        scratch_shapes=[
            pltpu.VMEM((2, D, WIDE), BF16),
            pltpu.VMEM((2, 256, D), BF16),
            pltpu.VMEM((2, 2, 4, 4, 16, D), BF16),
            pltpu.VMEM((2, 512, 2 * WIDE), F32),
            pltpu.VMEM((2, 512, 2 * WIDE), BF16),
            pltpu.VMEM((2, 2, 4, 1, 512), F32),
            pltpu.VMEM((2, 2, 9, 1, 512), F32),
            pltpu.VMEM((2, 1, 512), F32),
            pltpu.VMEM((2, 512, 128), F32),
            pltpu.VMEM((2, 512, 128), F32),
            pltpu.VMEM((2, 16, 1024), F32),
            *FFN_SCRATCH,
            *buffers,
            *stages,
            pltpu.SemaphoreType.DMA((copies,)),
            pltpu.SemaphoreType.DMA((copies,)),
            pltpu.SemaphoreType.DMA((7,)),
        ],
        compiler_params=pltpu.CompilerParams(
            collective_id=0, has_side_effects=True, vmem_limit_bytes=61 * 2**20
        ),
    )(frames_in, in_gain, out_gain, w_in, w_out, table, tail)


def shards(frames_in, in_gain, w_in, w_out, out_gain, table):
    tail = table[ROWS - REST :]
    mixed, log_total = fused(frames_in.T, in_gain[None], out_gain[None], w_in, w_out, table, tail)
    return (mixed.T, log_total.reshape(512))


def solution(mesh):
    placed = (
        P("frames", "hidden"),
        P(),
        P(None, "hidden"),
        P("hidden", None),
        P(),
        P(("frames", "hidden"), None),
    )
    return jax.shard_map(
        shards,
        mesh=mesh,
        in_specs=placed,
        out_specs=(P("frames", "hidden"), P("frames")),
        check_vma=False,
    )
```

```python
import functools
import math

import jax
import jax.numpy as jnp
from jax import lax
from jax.experimental import pallas as pl
from jax.experimental.pallas import tpu as pltpu
from jax.sharding import PartitionSpec as P

MESH = pl.DeviceIdType.MESH
D = 2048
ROWS = 1187
TAIL = 1168
REST = 32
AGAIN = REST - (ROWS - TAIL)
WIDE = 1280
SCORE = 1280
F32 = jnp.float32
BF16 = jnp.bfloat16
ALL = slice(None)


def coords():
    f = lax.axis_index("frames")
    h = lax.axis_index("hidden")
    return {
        "x": lax.rem(lax.div(h, 4), 4),
        "y": lax.div(h, 16) * 2 + lax.div(f, 2),
        "z": lax.rem(h, 4),
        "c": lax.rem(f, 2),
    }


def device(at):
    return (
        lax.rem(at["y"], 2) * 2 + at["c"],
        lax.div(at["y"], 2) * 16 + at["x"] * 4 + at["z"],
    )


def moved(me, dim, by):
    return device({**me, dim: lax.rem(me[dim] + by + 4, 4)})


class Links:
    def __init__(self, send_sems, recv_sems):
        self.send_sems, self.recv_sems = send_sems, recv_sems
        self.count, self.flying = 0, []

    def send(self, src, dst, to):
        copy = pltpu.make_async_remote_copy(
            src_ref=src,
            dst_ref=dst,
            send_sem=self.send_sems.at[self.count],
            recv_sem=self.recv_sems.at[self.count],
            device_id=to,
            device_id_type=MESH,
        )
        copy.start()
        self.count += 1
        self.flying.append(copy)
        return copy

    def drain(self):
        for copy in self.flying:
            copy.wait_send()
        self.flying = []


def run(*streams):
    streams = list(streams)
    while streams:
        for stream in list(streams):
            try:
                next(stream)
            except StopIteration:
                streams.remove(stream)


def gather_stream(links, me, buf, order, direct):
    for k, dim in enumerate(order):
        fixed = tuple(me[d] for d in reversed(order[k + 1 :]))
        i = me[dim]
        right, left = moved(me, dim, 1), moved(me, dim, -1)
        before, after = lax.rem(i + 3, 4), lax.rem(i + 1, 4)

        def go(j, part, to, fixed=fixed):
            cut = () if part is None else (slice(2 * part, 2 * part + 2),)
            block = buf.at[(*fixed, j, *cut)]
            return links.send(block, block, to)

        if direct[k]:
            copies = [go(i, None, to) for to in (moved(me, dim, 2), right, left)]
            yield
            for copy in copies:
                copy.wait_recv()
            continue
        r_low, l_high = go(i, 0, right), go(i, 1, left)
        r_high, l_low = go(i, 1, right), go(i, 0, left)
        yield
        r_low.wait_recv()
        r_far = go(before, 0, right)
        l_high.wait_recv()
        l_far = go(after, 1, left)
        yield
        for copy in (r_high, l_low, r_far, l_far):
            copy.wait_recv()


def add_stream(links, me, buf, stages, order, direct, result):
    for k, dim in enumerate(order):
        fixed = tuple(me[d] for d in order[:k])
        left_dims = len(order) - 1 - k
        i = me[dim]
        right, left = moved(me, dim, 1), moved(me, dim, -1)
        before, after, across = lax.rem(i + 3, 4), lax.rem(i + 1, 4), lax.rem(i + 2, 4)

        def view(j, part, fixed=fixed):
            cut = () if part is None else (slice(2 * part, 2 * part + 2),)
            return buf.at[(*fixed, j, *cut)]

        def add(j, at, sources, fixed=fixed, left_dims=left_dims):
            total = buf[(*fixed, j, *at)].astype(F32)
            for ref, lead in sources:
                total = total + ref[lead].astype(F32)
            if left_dims == 0:
                result(total)
            else:
                buf[(*fixed, j, *at)] = total.astype(buf.dtype)

        if direct[k]:
            (near,) = stages[k]
            copies = [
                links.send(view(j, None), near.at[n], to)
                for n, (j, to) in enumerate(
                    ((across, moved(me, dim, 2)), (after, right), (before, left))
                )
            ]
            yield
            for copy in copies:
                copy.wait_recv()
            add(i, () if left_dims else (ALL, ALL), [(near, (n,)) for n in range(3)])
            continue
        far, near = stages[k]
        r_far = links.send(view(across, 0), far.at[0], right)
        l_far = links.send(view(across, 1), far.at[1], left)
        r_high = links.send(view(after, 1), near.at[0, 2:4], right)
        l_low = links.send(view(before, 0), near.at[1, 0:2], left)
        yield
        r_far.wait_recv()
        for t in range(2):
            add(after, (t,), [(far, (0, t))])
        r_low = links.send(view(after, 0), near.at[0, 0:2], right)
        l_far.wait_recv()
        for t in range(2):
            add(before, (2 + t,), [(far, (1, t))])
        l_high = links.send(view(before, 1), near.at[1, 2:4], left)
        yield
        r_high.wait_recv()
        l_high.wait_recv()
        for t in (2, 3):
            add(i, (t,), [(near, (0, t)), (near, (1, t))])
        l_low.wait_recv()
        r_low.wait_recv()
        for t in (0, 1):
            add(i, (t,), [(near, (0, t)), (near, (1, t))])


def stage_shapes(direct, rows, width, dtype):
    shapes = []
    for k, straight in enumerate(direct):
        block = (4,) * (len(direct) - 1 - k)
        if not straight:
            shapes.append(pltpu.VMEM((2, 2, *block[1:], rows, width), dtype))
        shapes.append(pltpu.VMEM((3 if straight else 2, *block, rows, width), dtype))
    return shapes


def by_phase(direct, refs):
    refs = iter(refs)
    return [(next(refs),) if straight else (next(refs), next(refs)) for straight in direct]


def greet(peers):
    barrier = pltpu.get_barrier_semaphore()
    for peer in peers:
        pl.semaphore_signal(barrier, inc=1, device_id=peer, device_id_type=MESH)
    pl.semaphore_wait(barrier, len(peers))


FFN_ORDERS = ("xz", "zx")
FFN_GATHER, FFN_ADD = (True, True), (False, True)
GATHER, ADD = (True, True, False), (False, True, True)


def feed_forward(links, me, other_core, x_ref, gin_ref, gout_ref, w_hbm, loads, refs, beside, beside_done):
    xp, xs, win, wout, *refs = refs
    gathered, partial = refs[0:2], refs[2:4]
    n = (len(refs) - 4) // 2
    stages = [by_phase(FFN_ADD, refs[4 + n * k : 4 + n * k + n]) for k in range(2)]
    done = beside_done
    y_lo, half = lax.rem(me["y"], 2), lax.div(me["y"], 2)
    opposite = moved(me, "y", 2)
    cross = moved(me, "y", 2 * y_lo - 1)
    beside_y = moved(me, "y", 1 - 2 * y_lo)
    mine = y_lo * 2 + me["c"]

    def exchange_weights():
        theirs = (1 - y_lo) * 2 + me["c"]
        jobs = []
        for ref, hbm, rows, n in ((win, w_hbm[0], 512, 256), (wout, w_hbm[1], 64, 32)):
            for at in range(0, rows, n):
                own = pl.ds(pl.multiple_of(mine * rows + at, n), n)
                next_to = pl.ds(pl.multiple_of(theirs * rows + at, n), n)
                jobs.append((ref, hbm, own, next_to))

        def start(job):
            ref, hbm, own, next_to = job
            return links.send(hbm.at[next_to], ref.at[1, next_to], cross)

        got = [start(job) for job in jobs]
        passed, last = [], []

        def hand_over(n):
            ref, _, _, next_to = jobs[n]
            passed[n].wait_recv()
            last.append(links.send(ref.at[1, next_to], ref.at[1, next_to], other_core))

        def settle(what, *which):
            for n in which:
                last[n].wait_recv()
            done.add(what)

        for n, (ref, _, own, _) in enumerate(jobs):
            yield
            got[n].wait_recv()
            passed.append(links.send(ref.at[1, own], ref.at[1, own], beside_y))
            last.append(links.send(ref.at[1, own], ref.at[1, own], other_core))
            if n >= 1:
                hand_over(n - 1)
            if n == 3:
                settle("w_in", 0, 1, 2, 4)
        yield
        hand_over(len(jobs) - 1)
        yield
        settle("w_out", 3, 5, 6, 7)

    lanes = lax.broadcasted_iota(jnp.int32, (256, 128), 1) < 64

    def exchange_frames():
        xp[half] = jnp.concatenate([x_ref[:, 0:256], x_ref[:, 256:512]], axis=0).T
        got = links.send(xp.at[half], xp.at[half], opposite)
        yield
        got.wait_recv()
        p = [xp[0].astype(F32), xp[1].astype(F32)]
        r = [pltpu.roll(v, 64, 1) for v in p]
        first = half == 0
        block = jnp.where(
            lanes, jnp.where(first, p[0], r[0]), jnp.where(first, r[1], p[1])
        ).astype(BF16)
        for k, order in enumerate(FFN_ORDERS):
            gathered[k][me[order[1]], me[order[0]]] = block[128 * k : 128 * k + 128]
        streams = [gather_stream(links, me, gathered[k], o, FFN_GATHER) for k, o in enumerate(FFN_ORDERS)]
        while streams:
            for stream in list(streams):
                try:
                    next(stream)
                except StopIteration:
                    streams.remove(stream)
            if streams:
                yield
        done.add("frames")

    def compute():
        while "frames" not in done:
            yield
        few = lax.broadcasted_iota(jnp.int32, (128, 128), 1) < 64

        def unpack(p, squares):
            x, z = lax.div(p, 2), lax.rem(p, 2) * 2
            at = pl.multiple_of(p * 128, 128)
            sums = []
            for k in range(2):
                ref = gathered[k]
                a, b = (ref[z, x], ref[z + 1, x]) if k == 0 else (ref[x, z], ref[x, z + 1])
                a, b = a.astype(F32), b.astype(F32)
                rows = slice(128 * k, 128 * k + 128)
                top = jnp.where(few, a, pltpu.roll(b, 64, 1))
                low = jnp.where(few, pltpu.roll(a, 64, 1), b)
                xs[rows, pl.ds(at, 128)] = top.astype(BF16)
                xs[rows, pl.ds(at + 1024, 128)] = low.astype(BF16)
                sums.append(squares[k] + a * a + b * b)
            return tuple(sums)

        squares = lax.fori_loop(0, 8, unpack, (jnp.zeros((128, 128), F32),) * 2)
        mean_sq = jnp.sum(jnp.concatenate(squares, axis=0), axis=1, keepdims=True) * (1.0 / D)
        normed = (xs[...].astype(F32) * lax.rsqrt(mean_sq + 1e-06) * gin_ref[...]).astype(BF16)
        while "w_in" not in done:
            yield
        for load in loads:
            load.wait()
        hidden = [
            jax.nn.gelu(
                jnp.dot(normed, win[w], preferred_element_type=F32), approximate=True
            ).astype(BF16)
            for w in range(2)
        ]
        while "w_out" not in done:
            yield
        for k, order in enumerate(FFN_ORDERS):
            for part in range(2):
                cols = slice(1024 * k + 512 * part, 1024 * k + 512 * part + 512)
                block = jnp.dot(hidden[0], wout[0, :, cols], preferred_element_type=F32) + jnp.dot(
                    hidden[1], wout[1, :, cols], preferred_element_type=F32
                )
                for t in range(16):
                    at = (t // 4, t % 4) if order == "xz" else (t % 4, t // 4)
                    partial[k][(*at, ALL, slice(512 * part, 512 * part + 512))] = block[16 * t : 16 * t + 16]

    run(exchange_frames(), exchange_weights(), *beside, compute())
    found = {}
    run(
        *(
            add_stream(
                links, me, partial[k], stages[k], order, FFN_ADD,
                lambda value, k=k: found.update({k: value}),
            )
            for k, order in enumerate(FFN_ORDERS)
        )
    )
    row = pl.ds(pl.multiple_of(16 * (4 * me["x"] + me["z"]), 16), 16)
    total = jnp.concatenate([found[0], found[1]], axis=1)
    encoded = xs[row, :].astype(F32) + total
    mean_sq = jnp.mean(encoded * encoded, axis=1, keepdims=True)
    return (encoded * lax.rsqrt(mean_sq + 1e-06) * gout_ref[...]).astype(BF16)


FFN_SCRATCH = (
    [
        pltpu.VMEM((2, 256, 128), BF16),
        pltpu.VMEM((256, D), BF16),
        pltpu.VMEM((2, D, 256), BF16),
        pltpu.VMEM((2, 256, D), BF16),
    ]
    + [pltpu.VMEM((4, 4, 128, 128), BF16)] * 2
    + [pltpu.VMEM((4, 4, 16, 1024), F32)] * 2
    + stage_shapes(FFN_ADD, 16, 1024, F32) * 2
)
FFN_COPIES = 1 + 2 * (3 + 3) + 4 * 4 + 2 * (6 + 3)


ORDERS = ("xyz", "yzx", "zxy")
SPLITS = ((0, 384), (384, 384), (768, 256))


def kernel(
    x_ref, gin_ref, gout_ref, win_hbm, wout_hbm, table_hbm, tail_ref, out_ref, log_ref,
    turned, pieces, lat, scores, weights, stats, got_stats, sums, peaks, totals, fin,
    *rest,
):
    ffn_refs, rest = rest[: len(FFN_SCRATCH)], rest[len(FFN_SCRATCH) :]
    buffers = [rest[0:3], rest[3:6]]
    *stages, ssem, rsem, load_sem = rest[6:]
    me = coords()
    y_lo, y_hi = lax.rem(me["y"], 2), lax.div(me["y"], 2)
    load_in = pltpu.make_async_copy(win_hbm, ffn_refs[2].at[0], load_sem.at[0])
    load_out = pltpu.make_async_copy(wout_hbm, ffn_refs[3].at[0], load_sem.at[1])
    load_in.start()
    load_out.start()

    def load_piece(p):
        n = min(256, TAIL - 256 * p)
        copy = pltpu.make_async_copy(
            table_hbm.at[pl.ds(256 * p, n)], pieces.at[p % 2, pl.ds(0, n)], load_sem.at[2 + p]
        )
        copy.start()
        return copy

    coming = [load_piece(0), load_piece(1)]
    other_core = device({**me, "c": 1 - me["c"]})
    greet([moved(me, d, s) for d in ("x", "y", "z") for s in (1, -1, 2)] + [other_core])
    links = Links(ssem, rsem)
    swaps, weights_done = [], set()

    def turn_table():
        yield
        for p in range(5):
            coming[p].wait()
            if p == 4:
                pieces[0, TAIL - 1024 : TAIL + REST - 1024] = tail_ref[...]
                pieces[0, TAIL + REST - 1024 : 256] = jnp.zeros((WIDE - TAIL - REST, D), BF16)
            for q in range(2):
                block = pieces[p % 2, 128 * q : 128 * q + 128]
                at = 256 * p + 128 * q
                turned[0, :, at : at + 128] = block.T
            if p + 2 < 5:
                coming.append(load_piece(p + 2))
            if p < 4:
                yield
        while "w_out" not in weights_done:
            yield
        swaps.append(links.send(turned.at[0], turned.at[1], other_core))

    latent = feed_forward(
        links, me, other_core, x_ref, gin_ref, gout_ref, (win_hbm, wout_hbm), (load_in, load_out),
        ffn_refs, (turn_table(),), weights_done,
    )
    for s in range(2):
        for buf, order, (start, width) in zip(buffers[s], ORDERS, SPLITS):
            at = 1024 * s + start
            buf[tuple(me[d] for d in reversed(order))] = latent[:, at : at + width]

    done = set()

    def then(stream, *keys):
        yield from stream
        done.update(keys)

    def after(keys, stream):
        while not set(keys) <= done:
            yield
        yield from stream

    scale = 5.0 / math.sqrt(D) * math.log2(math.e)

    def collect():
        def block(t, _):
            at = {"y": lax.div(t, 16), "x": lax.rem(lax.div(t, 4), 4), "z": lax.rem(t, 4)}
            to = (lax.rem(at["y"], 2), lax.div(at["y"], 2), at["x"], at["z"])
            for s in range(2):
                for buf, order, (start, width) in zip(buffers[s], ORDERS, SPLITS):
                    cols = slice(1024 * s + start, 1024 * s + start + width)
                    lat[(*to, ALL, cols)] = buf[tuple(at[d] for d in reversed(order))]
            return 0

        lax.fori_loop(0, 64, block, 0)

    tile_lane = lax.broadcasted_iota(jnp.int32, (1, SCORE), 1)

    def score_tile(g, t):
        frames = lat[:, g].reshape(512, D)
        half, n = lax.div(t, WIDE // SCORE), lax.rem(t, WIDE // SCORE)
        cols = pl.ds(pl.multiple_of(n * SCORE, 128), SCORE)
        at = pl.ds(pl.multiple_of(t * SCORE, 128), SCORE)
        place = tile_lane + n * SCORE
        real = (place < TAIL) | ((place >= TAIL + AGAIN) & (place < TAIL + REST))
        product = jnp.dot(frames, turned[half, :, cols], preferred_element_type=F32)
        value = jnp.where(real, product * scale, -1e30)
        scores[g, :, at] = value
        peaks[g] = functools.reduce(
            jnp.maximum, [peaks[g]] + [value[:, c : c + 128] for c in range(0, SCORE, 128)]
        )

    def find_peaks(g):
        peaks[g] = jnp.broadcast_to(jnp.max(peaks[g], axis=1, keepdims=True), (512, 128))
        totals[g] = jnp.zeros((512, 128), F32)

    def weigh(g, rows, first, tiles):
        top = peaks[g, rows]
        total = totals[g, rows]
        for c in range(tiles):
            at = pl.ds(pl.multiple_of(first + 128 * c, 128), 128)
            e = jnp.exp2(scores[g, rows, at] - top)
            weights[g, rows, at] = e.astype(BF16)
            total = total + e
        totals[g, rows] = total

    def local_top(g):
        stats[0, g, 0, 0:1] = peaks[g].T[0:1]
        done.add(f"peak{g}")

    def local_sum(g):
        total = jnp.broadcast_to(jnp.sum(totals[g], axis=1, keepdims=True), (512, 128))
        sums[g] = total.T[0:1]

    def loop(first, last, *bodies):
        def step(t, _):
            for body in bodies:
                body(t)
            return 0

        lax.fori_loop(first, last, step, 0)

    def share(g, kind, combine):
        for phase, dim in enumerate("xyz"):
            copies = [
                links.send(
                    stats.at[kind, g, phase], got_stats.at[kind, g, 3 * phase + n], moved(me, dim, s)
                )
                for n, s in enumerate((1, -1, 2))
            ]
            yield
            for copy in copies:
                copy.wait_recv()
            parts = [stats[kind, g, phase]] + [got_stats[kind, g, 3 * phase + n] for n in range(3)]
            stats[kind, g, phase + 1] = functools.reduce(combine, parts)

    def share_sum(g):
        stats[1, g, 0, 0:1] = sums[g] * jnp.exp2(stats[0, g, 0, 0:1] - stats[0, g, 3, 0:1])
        yield from share(g, 1, jnp.add)

    def mix_tile(g, t):
        rows = pl.ds(pl.multiple_of(t * 1024, 1024), 1024)
        dims = (((1,), (1,)), ((), ()))
        total = lax.dot_general(
            turned[0, rows, :], weights[g, :, 0:WIDE], dims, preferred_element_type=F32
        ) + lax.dot_general(
            turned[1, rows, :], weights[g, :, WIDE:], dims, preferred_element_type=F32
        )
        for n in range(2):
            lanes = pl.ds(pl.multiple_of(t * 1024 + 512 * n, 512), 512)
            scores[g, :, lanes] = total[512 * n : 512 * n + 512]

    def rescale(g):
        factor = jnp.exp2(stats[0, g, 0, 0:1] - stats[0, g, 3, 0:1])

        def block(h8, _):
            for n in range(4):
                h = 8 * n + h8
                y_up, x, z = lax.div(h, 16), lax.rem(lax.div(h, 4), 4), lax.rem(h, 4)
                for yl in range(2):
                    at = {"x": x, "y": 2 * y_up + yl, "z": z}
                    for buf, order, (start, width) in zip(buffers[g], ORDERS, SPLITS):
                        for c in range(width // 128):
                            unit = start // 128 + c
                            lane = 256 * yl + 128 * (unit % 2)
                            rows = pl.ds(pl.multiple_of(h8 * 64 + 16 * (unit // 2), 16), 16)
                            value = scores[g, rows, 512 * n + lane : 512 * n + lane + 128]
                            buf[(*(at[d] for d in order), ALL, slice(128 * c, 128 * c + 128))] = (
                                value * factor[:, lane : lane + 128]
                            ).astype(BF16)
            return 0

        lax.fori_loop(0, 8, block, 0)

    def wait_for(*keys):
        while not set(keys) <= done:
            yield

    def compute():
        yield from wait_for(*(f"lat{s}{k}" for s in range(2) for k in range(3)))
        swaps[0].wait_recv()
        collect()
        links.drain()
        peaks[...] = jnp.full((2, 512, 128), -1e30, F32)
        tiles = 2 * WIDE // SCORE
        loop(0, tiles, functools.partial(score_tile, 0))
        find_peaks(0)
        local_top(0)
        yield
        loop(
            0, tiles, functools.partial(score_tile, 1),
            lambda t: weigh(0, ALL, t * SCORE, SCORE // 128),
        )
        local_sum(0)
        find_peaks(1)
        local_top(1)
        yield
        for part in range(2):
            loop(
                part, part + 1, functools.partial(mix_tile, 0),
                lambda t: weigh(1, pl.ds(pl.multiple_of(t * 256, 256), 256), 0, 20),
            )
            if part == 1:
                local_sum(1)
            yield
        yield from wait_for("stats0")
        rescale(0)
        done.add("sums0")
        yield
        for part in range(2):
            loop(part, part + 1, functools.partial(mix_tile, 1))
        yield from wait_for("stats1")
        rescale(1)
        done.add("sums1")

    def final():
        for g in range(2):
            yield from wait_for(f"total{g}", *(f"out{g}{k}" for k in range(3)))
            lanes = pl.ds(pl.multiple_of(y_lo * 256, 256), 256)
            top, total = stats[0, g, 3, 0:1, lanes], stats[1, g, 3, 0:1, lanes]
            for j in range(4):
                out_ref[16 * j : 16 * j + 16, 256 * g : 256 * g + 256] = (
                    fin[g, :, 256 * j : 256 * j + 256] / total
                ).astype(BF16)
            log_ref[:, 256 * g : 256 * g + 256] = top * math.log(2.0) + jnp.log(total)

    streams = [
        then(gather_stream(links, me, buffers[s][k], o, GATHER), f"lat{s}{k}")
        for s in range(2)
        for k, o in enumerate(ORDERS)
    ]
    streams.append(compute())
    for g in range(2):
        streams.append(then(after([f"peak{g}"], share(g, 0, jnp.maximum)), f"stats{g}"))
        streams.append(then(after([f"sums{g}"], share_sum(g)), f"total{g}"))
    for g in range(2):
        for k, (o, (start, width)) in enumerate(zip(ORDERS, SPLITS)):
            def result(value, g=g, start=start, width=width):
                fin[g, :, start : start + width] = value

            n = len(stages) // 6
            at = n * (3 * g + k)
            stream = add_stream(
                links, me, buffers[g][k], by_phase(ADD, stages[at : at + n]), o, ADD, result
            )
            streams.append(then(after([f"sums{g}"], stream), f"out{g}{k}"))
    streams.append(final())
    run(*streams)
    links.drain()


def fused(frames_in, in_gain, out_gain, w_in, w_out, table, tail):
    vmem = pl.BlockSpec(memory_space=pltpu.VMEM)
    hbm = pl.BlockSpec(memory_space=pl.ANY)
    copies = FFN_COPIES + 1 + 2 * 18 + 2 * 3 * 2 * 12
    buffers, stages = [], []
    for _ in range(2):
        for _, width in SPLITS:
            buffers.append(pltpu.VMEM((4, 4, 4, 16, width), BF16))
            stages += stage_shapes(ADD, 16, width, BF16)
    return pl.pallas_call(
        kernel,
        out_shape=(
            jax.ShapeDtypeStruct((64, 512), BF16),
            jax.ShapeDtypeStruct((1, 512), F32),
        ),
        in_specs=[vmem] * 3 + [hbm] * 3 + [vmem],
        out_specs=(vmem, vmem),
        scratch_shapes=[
            pltpu.VMEM((2, D, WIDE), BF16),
            pltpu.VMEM((2, 256, D), BF16),
            pltpu.VMEM((2, 2, 4, 4, 16, D), BF16),
            pltpu.VMEM((2, 512, 2 * WIDE), F32),
            pltpu.VMEM((2, 512, 2 * WIDE), BF16),
            pltpu.VMEM((2, 2, 4, 1, 512), F32),
            pltpu.VMEM((2, 2, 9, 1, 512), F32),
            pltpu.VMEM((2, 1, 512), F32),
            pltpu.VMEM((2, 512, 128), F32),
            pltpu.VMEM((2, 512, 128), F32),
            pltpu.VMEM((2, 16, 1024), F32),
            *FFN_SCRATCH,
            *buffers,
            *stages,
            pltpu.SemaphoreType.DMA((copies,)),
            pltpu.SemaphoreType.DMA((copies,)),
            pltpu.SemaphoreType.DMA((7,)),
        ],
        compiler_params=pltpu.CompilerParams(
            collective_id=0, has_side_effects=True, vmem_limit_bytes=61 * 2**20
        ),
    )(frames_in, in_gain, out_gain, w_in, w_out, table, tail)


def shards(frames_in, in_gain, w_in, w_out, out_gain, table):
    tail = table[ROWS - REST :]
    mixed, log_total = fused(frames_in.T, in_gain[None], out_gain[None], w_in, w_out, table, tail)
    return (mixed.T, log_total.reshape(512))


def solution(mesh):
    placed = (
        P("frames", "hidden"),
        P(),
        P(None, "hidden"),
        P("hidden", None),
        P(),
        P(("frames", "hidden"), None),
    )
    return jax.shard_map(
        shards,
        mesh=mesh,
        in_specs=placed,
        out_specs=(P("frames", "hidden"), P("frames")),
        check_vma=False,
    )
```

```python
import functools
import math

import jax
import jax.numpy as jnp
from jax import lax
from jax.experimental import pallas as pl
from jax.experimental.pallas import tpu as pltpu
from jax.sharding import PartitionSpec as P

MESH = pl.DeviceIdType.MESH
D = 2048
ROWS = 1187
TAIL = 1168
REST = 32
AGAIN = REST - (ROWS - TAIL)
WIDE = 1280
SCORE = 1280
F32 = jnp.float32
BF16 = jnp.bfloat16
ALL = slice(None)


def coords():
    f = lax.axis_index("frames")
    h = lax.axis_index("hidden")
    return {
        "x": lax.rem(lax.div(h, 4), 4),
        "y": lax.div(h, 16) * 2 + lax.div(f, 2),
        "z": lax.rem(h, 4),
        "c": lax.rem(f, 2),
    }


def device(at):
    return (
        lax.rem(at["y"], 2) * 2 + at["c"],
        lax.div(at["y"], 2) * 16 + at["x"] * 4 + at["z"],
    )


def moved(me, dim, by):
    return device({**me, dim: lax.rem(me[dim] + by + 4, 4)})


class Links:
    def __init__(self, send_sems, recv_sems):
        self.send_sems, self.recv_sems = send_sems, recv_sems
        self.count, self.flying = 0, []

    def send(self, src, dst, to):
        copy = pltpu.make_async_remote_copy(
            src_ref=src,
            dst_ref=dst,
            send_sem=self.send_sems.at[self.count],
            recv_sem=self.recv_sems.at[self.count],
            device_id=to,
            device_id_type=MESH,
        )
        copy.start()
        self.count += 1
        self.flying.append(copy)
        return copy

    def drain(self):
        for copy in self.flying:
            copy.wait_send()
        self.flying = []


def run(*streams):
    streams = list(streams)
    while streams:
        for stream in list(streams):
            try:
                next(stream)
            except StopIteration:
                streams.remove(stream)


def gather_stream(links, me, buf, order, direct):
    for k, dim in enumerate(order):
        fixed = tuple(me[d] for d in reversed(order[k + 1 :]))
        i = me[dim]
        right, left = moved(me, dim, 1), moved(me, dim, -1)
        before, after = lax.rem(i + 3, 4), lax.rem(i + 1, 4)

        def go(j, part, to, fixed=fixed):
            cut = () if part is None else (slice(2 * part, 2 * part + 2),)
            block = buf.at[(*fixed, j, *cut)]
            return links.send(block, block, to)

        if direct[k]:
            copies = [go(i, None, to) for to in (moved(me, dim, 2), right, left)]
            yield
            for copy in copies:
                copy.wait_recv()
            continue
        r_low, l_high = go(i, 0, right), go(i, 1, left)
        r_high, l_low = go(i, 1, right), go(i, 0, left)
        yield
        r_low.wait_recv()
        r_far = go(before, 0, right)
        l_high.wait_recv()
        l_far = go(after, 1, left)
        yield
        for copy in (r_high, l_low, r_far, l_far):
            copy.wait_recv()


def add_stream(links, me, buf, stages, order, direct, result):
    for k, dim in enumerate(order):
        fixed = tuple(me[d] for d in order[:k])
        left_dims = len(order) - 1 - k
        i = me[dim]
        right, left = moved(me, dim, 1), moved(me, dim, -1)
        before, after, across = lax.rem(i + 3, 4), lax.rem(i + 1, 4), lax.rem(i + 2, 4)

        def view(j, part, fixed=fixed):
            cut = () if part is None else (slice(2 * part, 2 * part + 2),)
            return buf.at[(*fixed, j, *cut)]

        def add(j, at, sources, fixed=fixed, left_dims=left_dims):
            total = buf[(*fixed, j, *at)].astype(F32)
            for ref, lead in sources:
                total = total + ref[lead].astype(F32)
            if left_dims == 0:
                result(total)
            else:
                buf[(*fixed, j, *at)] = total.astype(buf.dtype)

        if direct[k]:
            (near,) = stages[k]
            copies = [
                links.send(view(j, None), near.at[n], to)
                for n, (j, to) in enumerate(
                    ((across, moved(me, dim, 2)), (after, right), (before, left))
                )
            ]
            yield
            for copy in copies:
                copy.wait_recv()
            add(i, () if left_dims else (ALL, ALL), [(near, (n,)) for n in range(3)])
            continue
        far, near = stages[k]
        r_far = links.send(view(across, 0), far.at[0], right)
        l_far = links.send(view(across, 1), far.at[1], left)
        r_high = links.send(view(after, 1), near.at[0, 2:4], right)
        l_low = links.send(view(before, 0), near.at[1, 0:2], left)
        yield
        r_far.wait_recv()
        for t in range(2):
            add(after, (t,), [(far, (0, t))])
        r_low = links.send(view(after, 0), near.at[0, 0:2], right)
        l_far.wait_recv()
        for t in range(2):
            add(before, (2 + t,), [(far, (1, t))])
        l_high = links.send(view(before, 1), near.at[1, 2:4], left)
        yield
        r_high.wait_recv()
        l_high.wait_recv()
        for t in (2, 3):
            add(i, (t,), [(near, (0, t)), (near, (1, t))])
        l_low.wait_recv()
        r_low.wait_recv()
        for t in (0, 1):
            add(i, (t,), [(near, (0, t)), (near, (1, t))])


def stage_shapes(direct, rows, width, dtype):
    shapes = []
    for k, straight in enumerate(direct):
        block = (4,) * (len(direct) - 1 - k)
        if not straight:
            shapes.append(pltpu.VMEM((2, 2, *block[1:], rows, width), dtype))
        shapes.append(pltpu.VMEM((3 if straight else 2, *block, rows, width), dtype))
    return shapes


def by_phase(direct, refs):
    refs = iter(refs)
    return [(next(refs),) if straight else (next(refs), next(refs)) for straight in direct]


def greet(peers):
    barrier = pltpu.get_barrier_semaphore()
    for peer in peers:
        pl.semaphore_signal(barrier, inc=1, device_id=peer, device_id_type=MESH)
    pl.semaphore_wait(barrier, len(peers))


FFN_ORDERS = ("xz", "zx")
FFN_GATHER, FFN_ADD = (True, True), (False, True)
GATHER, ADD = (True, True, False), (False, True, True)


def feed_forward(links, me, other_core, x_ref, gin_ref, gout_ref, w_hbm, loads, refs, beside, beside_done):
    xp, xs, win, wout, *refs = refs
    gathered, partial = refs[0:2], refs[2:4]
    n = (len(refs) - 4) // 2
    stages = [by_phase(FFN_ADD, refs[4 + n * k : 4 + n * k + n]) for k in range(2)]
    done = beside_done
    y_lo, half = lax.rem(me["y"], 2), lax.div(me["y"], 2)
    opposite = moved(me, "y", 2)
    cross = moved(me, "y", 2 * y_lo - 1)
    beside_y = moved(me, "y", 1 - 2 * y_lo)
    mine = y_lo * 2 + me["c"]

    def exchange_weights():
        theirs = (1 - y_lo) * 2 + me["c"]
        jobs = []
        for ref, hbm, rows, n in ((win, w_hbm[0], 512, 256), (wout, w_hbm[1], 64, 32)):
            for at in range(0, rows, n):
                own = pl.ds(pl.multiple_of(mine * rows + at, n), n)
                next_to = pl.ds(pl.multiple_of(theirs * rows + at, n), n)
                jobs.append((ref, hbm, own, next_to))

        def start(job):
            ref, hbm, own, next_to = job
            return links.send(hbm.at[next_to], ref.at[1, next_to], cross)

        got = [start(job) for job in jobs]
        passed, last = [], []

        def hand_over(n):
            ref, _, _, next_to = jobs[n]
            passed[n].wait_recv()
            last.append(links.send(ref.at[1, next_to], ref.at[1, next_to], other_core))

        def settle(what, *which):
            for n in which:
                last[n].wait_recv()
            done.add(what)

        for n, (ref, _, own, _) in enumerate(jobs):
            yield
            got[n].wait_recv()
            passed.append(links.send(ref.at[1, own], ref.at[1, own], beside_y))
            last.append(links.send(ref.at[1, own], ref.at[1, own], other_core))
            if n >= 1:
                hand_over(n - 1)
            if n == 3:
                settle("w_in", 0, 1, 2, 4)
        yield
        hand_over(len(jobs) - 1)
        yield
        settle("w_out", 3, 5, 6, 7)

    lanes = lax.broadcasted_iota(jnp.int32, (256, 128), 1) < 64

    def exchange_frames():
        xp[half] = jnp.concatenate([x_ref[:, 0:256], x_ref[:, 256:512]], axis=0).T
        got = links.send(xp.at[half], xp.at[half], opposite)
        yield
        got.wait_recv()
        p = [xp[0].astype(F32), xp[1].astype(F32)]
        r = [pltpu.roll(v, 64, 1) for v in p]
        first = half == 0
        block = jnp.where(
            lanes, jnp.where(first, p[0], r[0]), jnp.where(first, r[1], p[1])
        ).astype(BF16)
        for k, order in enumerate(FFN_ORDERS):
            gathered[k][me[order[1]], me[order[0]]] = block[128 * k : 128 * k + 128]
        streams = [gather_stream(links, me, gathered[k], o, FFN_GATHER) for k, o in enumerate(FFN_ORDERS)]
        while streams:
            for stream in list(streams):
                try:
                    next(stream)
                except StopIteration:
                    streams.remove(stream)
            if streams:
                yield
        done.add("frames")

    def compute():
        while "frames" not in done:
            yield
        few = lax.broadcasted_iota(jnp.int32, (128, 128), 1) < 64

        def unpack(p, squares):
            x, z = lax.div(p, 2), lax.rem(p, 2) * 2
            at = pl.multiple_of(p * 128, 128)
            sums = []
            for k in range(2):
                ref = gathered[k]
                a, b = (ref[z, x], ref[z + 1, x]) if k == 0 else (ref[x, z], ref[x, z + 1])
                a, b = a.astype(F32), b.astype(F32)
                rows = slice(128 * k, 128 * k + 128)
                top = jnp.where(few, a, pltpu.roll(b, 64, 1))
                low = jnp.where(few, pltpu.roll(a, 64, 1), b)
                xs[rows, pl.ds(at, 128)] = top.astype(BF16)
                xs[rows, pl.ds(at + 1024, 128)] = low.astype(BF16)
                sums.append(squares[k] + a * a + b * b)
            return tuple(sums)

        squares = lax.fori_loop(0, 8, unpack, (jnp.zeros((128, 128), F32),) * 2)
        mean_sq = jnp.sum(jnp.concatenate(squares, axis=0), axis=1, keepdims=True) * (1.0 / D)
        normed = (xs[...].astype(F32) * lax.rsqrt(mean_sq + 1e-06) * gin_ref[...]).astype(BF16)
        while "w_in" not in done:
            yield
        for load in loads:
            load.wait()
        hidden = [
            jax.nn.gelu(
                jnp.dot(normed, win[w], preferred_element_type=F32), approximate=True
            ).astype(BF16)
            for w in range(2)
        ]
        while "w_out" not in done:
            yield
        for k, order in enumerate(FFN_ORDERS):
            for part in range(2):
                cols = slice(1024 * k + 512 * part, 1024 * k + 512 * part + 512)
                block = jnp.dot(hidden[0], wout[0, :, cols], preferred_element_type=F32) + jnp.dot(
                    hidden[1], wout[1, :, cols], preferred_element_type=F32
                )
                for t in range(16):
                    at = (t // 4, t % 4) if order == "xz" else (t % 4, t // 4)
                    partial[k][(*at, ALL, slice(512 * part, 512 * part + 512))] = block[16 * t : 16 * t + 16]

    run(exchange_frames(), exchange_weights(), *beside, compute())
    found = {}
    run(
        *(
            add_stream(
                links, me, partial[k], stages[k], order, FFN_ADD,
                lambda value, k=k: found.update({k: value}),
            )
            for k, order in enumerate(FFN_ORDERS)
        )
    )
    row = pl.ds(pl.multiple_of(16 * (4 * me["x"] + me["z"]), 16), 16)
    total = jnp.concatenate([found[0], found[1]], axis=1)
    encoded = xs[row, :].astype(F32) + total
    mean_sq = jnp.mean(encoded * encoded, axis=1, keepdims=True)
    return (encoded * lax.rsqrt(mean_sq + 1e-06) * gout_ref[...]).astype(BF16)


FFN_SCRATCH = (
    [
        pltpu.VMEM((2, 256, 128), BF16),
        pltpu.VMEM((256, D), BF16),
        pltpu.VMEM((2, D, 256), BF16),
        pltpu.VMEM((2, 256, D), BF16),
    ]
    + [pltpu.VMEM((4, 4, 128, 128), BF16)] * 2
    + [pltpu.VMEM((4, 4, 16, 1024), F32)] * 2
    + stage_shapes(FFN_ADD, 16, 1024, F32) * 2
)
FFN_COPIES = 1 + 2 * (3 + 3) + 4 * 4 + 2 * (6 + 3)


ORDERS = ("xyz", "yzx", "zxy")
SPLITS = ((0, 384), (384, 384), (768, 256))


def kernel(
    x_ref, gin_ref, gout_ref, win_hbm, wout_hbm, table_hbm, tail_ref, out_ref, log_ref,
    turned, pieces, lat, scores, weights, stats, got_stats, sums, peaks, totals, fin,
    *rest,
):
    ffn_refs, rest = rest[: len(FFN_SCRATCH)], rest[len(FFN_SCRATCH) :]
    buffers = [rest[0:3], rest[3:6]]
    *stages, ssem, rsem, load_sem = rest[6:]
    me = coords()
    y_lo, y_hi = lax.rem(me["y"], 2), lax.div(me["y"], 2)
    load_in = pltpu.make_async_copy(win_hbm, ffn_refs[2].at[0], load_sem.at[0])
    load_out = pltpu.make_async_copy(wout_hbm, ffn_refs[3].at[0], load_sem.at[1])
    load_in.start()
    load_out.start()

    def load_piece(p):
        n = min(256, TAIL - 256 * p)
        copy = pltpu.make_async_copy(
            table_hbm.at[pl.ds(256 * p, n)], pieces.at[p % 2, pl.ds(0, n)], load_sem.at[2 + p]
        )
        copy.start()
        return copy

    coming = [load_piece(0), load_piece(1)]
    other_core = device({**me, "c": 1 - me["c"]})
    greet([moved(me, d, s) for d in ("x", "y", "z") for s in (1, -1, 2)] + [other_core])
    links = Links(ssem, rsem)
    swaps, weights_done = [], set()

    def turn_table():
        yield
        for p in range(5):
            coming[p].wait()
            if p == 4:
                pieces[0, TAIL - 1024 : TAIL + REST - 1024] = tail_ref[...]
                pieces[0, TAIL + REST - 1024 : 256] = jnp.zeros((WIDE - TAIL - REST, D), BF16)
            for q in range(2):
                block = pieces[p % 2, 128 * q : 128 * q + 128]
                at = 256 * p + 128 * q
                turned[0, :, at : at + 128] = block.T
            if p + 2 < 5:
                coming.append(load_piece(p + 2))
            if p < 4:
                yield
        while "w_out" not in weights_done:
            yield
        swaps.append(links.send(turned.at[0], turned.at[1], other_core))

    latent = feed_forward(
        links, me, other_core, x_ref, gin_ref, gout_ref, (win_hbm, wout_hbm), (load_in, load_out),
        ffn_refs, (turn_table(),), weights_done,
    )
    for s in range(2):
        for buf, order, (start, width) in zip(buffers[s], ORDERS, SPLITS):
            at = 1024 * s + start
            buf[tuple(me[d] for d in reversed(order))] = latent[:, at : at + width]

    done = set()

    def then(stream, *keys):
        yield from stream
        done.update(keys)

    def after(keys, stream):
        while not set(keys) <= done:
            yield
        yield from stream

    scale = 5.0 / math.sqrt(D) * math.log2(math.e)

    def collect():
        def block(t, _):
            at = {"y": lax.div(t, 16), "x": lax.rem(lax.div(t, 4), 4), "z": lax.rem(t, 4)}
            to = (lax.rem(at["y"], 2), lax.div(at["y"], 2), at["x"], at["z"])
            for s in range(2):
                for buf, order, (start, width) in zip(buffers[s], ORDERS, SPLITS):
                    cols = slice(1024 * s + start, 1024 * s + start + width)
                    lat[(*to, ALL, cols)] = buf[tuple(at[d] for d in reversed(order))]
            return 0

        lax.fori_loop(0, 64, block, 0)

    tile_lane = lax.broadcasted_iota(jnp.int32, (1, SCORE), 1)

    def score_tile(g, t):
        frames = lat[:, g].reshape(512, D)
        half, n = lax.div(t, WIDE // SCORE), lax.rem(t, WIDE // SCORE)
        cols = pl.ds(pl.multiple_of(n * SCORE, 128), SCORE)
        at = pl.ds(pl.multiple_of(t * SCORE, 128), SCORE)
        place = tile_lane + n * SCORE
        real = (place < TAIL) | ((place >= TAIL + AGAIN) & (place < TAIL + REST))
        product = jnp.dot(frames, turned[half, :, cols], preferred_element_type=F32)
        value = jnp.where(real, product * scale, -1e30)
        scores[g, :, at] = value
        peaks[g] = functools.reduce(
            jnp.maximum, [peaks[g]] + [value[:, c : c + 128] for c in range(0, SCORE, 128)]
        )

    def find_peaks(g):
        peaks[g] = jnp.broadcast_to(jnp.max(peaks[g], axis=1, keepdims=True), (512, 128))
        totals[g] = jnp.zeros((512, 128), F32)

    def weigh(g, rows, first, tiles):
        top = peaks[g, rows]
        total = totals[g, rows]
        for c in range(tiles):
            at = pl.ds(pl.multiple_of(first + 128 * c, 128), 128)
            e = jnp.exp2(scores[g, rows, at] - top)
            weights[g, rows, at] = e.astype(BF16)
            total = total + e
        totals[g, rows] = total

    def local_top(g):
        stats[0, g, 0, 0:1] = peaks[g].T[0:1]
        done.add(f"peak{g}")

    def local_sum(g):
        total = jnp.broadcast_to(jnp.sum(totals[g], axis=1, keepdims=True), (512, 128))
        sums[g] = total.T[0:1]

    def loop(first, last, *bodies):
        def step(t, _):
            for body in bodies:
                body(t)
            return 0

        lax.fori_loop(first, last, step, 0)

    def share(g, kind, combine):
        for phase, dim in enumerate("xyz"):
            copies = [
                links.send(
                    stats.at[kind, g, phase], got_stats.at[kind, g, 3 * phase + n], moved(me, dim, s)
                )
                for n, s in enumerate((1, -1, 2))
            ]
            yield
            for copy in copies:
                copy.wait_recv()
            parts = [stats[kind, g, phase]] + [got_stats[kind, g, 3 * phase + n] for n in range(3)]
            stats[kind, g, phase + 1] = functools.reduce(combine, parts)

    def share_sum(g):
        stats[1, g, 0, 0:1] = sums[g] * jnp.exp2(stats[0, g, 0, 0:1] - stats[0, g, 3, 0:1])
        yield from share(g, 1, jnp.add)

    def mix_tile(g, t):
        rows = pl.ds(pl.multiple_of(t * 1024, 1024), 1024)
        dims = (((1,), (1,)), ((), ()))
        total = lax.dot_general(
            turned[0, rows, :], weights[g, :, 0:WIDE], dims, preferred_element_type=F32
        ) + lax.dot_general(
            turned[1, rows, :], weights[g, :, WIDE:], dims, preferred_element_type=F32
        )
        for n in range(2):
            lanes = pl.ds(pl.multiple_of(t * 1024 + 512 * n, 512), 512)
            scores[g, :, lanes] = total[512 * n : 512 * n + 512]

    def rescale(g):
        factor = jnp.exp2(stats[0, g, 0, 0:1] - stats[0, g, 3, 0:1])

        def block(h8, _):
            for n in range(4):
                h = 8 * n + h8
                y_up, x, z = lax.div(h, 16), lax.rem(lax.div(h, 4), 4), lax.rem(h, 4)
                for yl in range(2):
                    at = {"x": x, "y": 2 * y_up + yl, "z": z}
                    for buf, order, (start, width) in zip(buffers[g], ORDERS, SPLITS):
                        for c in range(width // 128):
                            unit = start // 128 + c
                            lane = 256 * yl + 128 * (unit % 2)
                            rows = pl.ds(pl.multiple_of(h8 * 64 + 16 * (unit // 2), 16), 16)
                            value = scores[g, rows, 512 * n + lane : 512 * n + lane + 128]
                            buf[(*(at[d] for d in order), ALL, slice(128 * c, 128 * c + 128))] = (
                                value * factor[:, lane : lane + 128]
                            ).astype(BF16)
            return 0

        lax.fori_loop(0, 8, block, 0)

    def wait_for(*keys):
        while not set(keys) <= done:
            yield

    def compute():
        yield from wait_for(*(f"lat{s}{k}" for s in range(2) for k in range(3)))
        swaps[0].wait_recv()
        collect()
        peaks[...] = jnp.full((2, 512, 128), -1e30, F32)
        tiles = 2 * WIDE // SCORE
        loop(0, tiles, functools.partial(score_tile, 0))
        find_peaks(0)
        local_top(0)
        yield
        loop(
            0, tiles, functools.partial(score_tile, 1),
            lambda t: weigh(0, ALL, t * SCORE, SCORE // 128),
        )
        local_sum(0)
        find_peaks(1)
        local_top(1)
        yield
        for part in range(2):
            loop(
                part, part + 1, functools.partial(mix_tile, 0),
                lambda t: weigh(1, pl.ds(pl.multiple_of(t * 256, 256), 256), 0, 20),
            )
            if part == 1:
                local_sum(1)
            yield
        yield from wait_for("stats0")
        links.drain()
        rescale(0)
        done.add("sums0")
        yield
        for part in range(2):
            loop(part, part + 1, functools.partial(mix_tile, 1))
        yield from wait_for("stats1")
        rescale(1)
        done.add("sums1")

    def final():
        for g in range(2):
            yield from wait_for(f"total{g}", *(f"out{g}{k}" for k in range(3)))
            lanes = pl.ds(pl.multiple_of(y_lo * 256, 256), 256)
            top, total = stats[0, g, 3, 0:1, lanes], stats[1, g, 3, 0:1, lanes]
            for j in range(4):
                out_ref[16 * j : 16 * j + 16, 256 * g : 256 * g + 256] = (
                    fin[g, :, 256 * j : 256 * j + 256] / total
                ).astype(BF16)
            log_ref[:, 256 * g : 256 * g + 256] = top * math.log(2.0) + jnp.log(total)

    streams = [
        then(gather_stream(links, me, buffers[s][k], o, GATHER), f"lat{s}{k}")
        for s in range(2)
        for k, o in enumerate(ORDERS)
    ]
    streams.append(compute())
    for g in range(2):
        streams.append(then(after([f"peak{g}"], share(g, 0, jnp.maximum)), f"stats{g}"))
        streams.append(then(after([f"sums{g}"], share_sum(g)), f"total{g}"))
    for g in range(2):
        for k, (o, (start, width)) in enumerate(zip(ORDERS, SPLITS)):
            def result(value, g=g, start=start, width=width):
                fin[g, :, start : start + width] = value

            n = len(stages) // 6
            at = n * (3 * g + k)
            stream = add_stream(
                links, me, buffers[g][k], by_phase(ADD, stages[at : at + n]), o, ADD, result
            )
            streams.append(then(after([f"sums{g}"], stream), f"out{g}{k}"))
    streams.append(final())
    run(*streams)
    links.drain()


def fused(frames_in, in_gain, out_gain, w_in, w_out, table, tail):
    vmem = pl.BlockSpec(memory_space=pltpu.VMEM)
    hbm = pl.BlockSpec(memory_space=pl.ANY)
    copies = FFN_COPIES + 1 + 2 * 18 + 2 * 3 * 2 * 12
    buffers, stages = [], []
    for _ in range(2):
        for _, width in SPLITS:
            buffers.append(pltpu.VMEM((4, 4, 4, 16, width), BF16))
            stages += stage_shapes(ADD, 16, width, BF16)
    return pl.pallas_call(
        kernel,
        out_shape=(
            jax.ShapeDtypeStruct((64, 512), BF16),
            jax.ShapeDtypeStruct((1, 512), F32),
        ),
        in_specs=[vmem] * 3 + [hbm] * 3 + [vmem],
        out_specs=(vmem, vmem),
        scratch_shapes=[
            pltpu.VMEM((2, D, WIDE), BF16),
            pltpu.VMEM((2, 256, D), BF16),
            pltpu.VMEM((2, 2, 4, 4, 16, D), BF16),
            pltpu.VMEM((2, 512, 2 * WIDE), F32),
            pltpu.VMEM((2, 512, 2 * WIDE), BF16),
            pltpu.VMEM((2, 2, 4, 1, 512), F32),
            pltpu.VMEM((2, 2, 9, 1, 512), F32),
            pltpu.VMEM((2, 1, 512), F32),
            pltpu.VMEM((2, 512, 128), F32),
            pltpu.VMEM((2, 512, 128), F32),
            pltpu.VMEM((2, 16, 1024), F32),
            *FFN_SCRATCH,
            *buffers,
            *stages,
            pltpu.SemaphoreType.DMA((copies,)),
            pltpu.SemaphoreType.DMA((copies,)),
            pltpu.SemaphoreType.DMA((7,)),
        ],
        compiler_params=pltpu.CompilerParams(
            collective_id=0, has_side_effects=True, vmem_limit_bytes=61 * 2**20
        ),
    )(frames_in, in_gain, out_gain, w_in, w_out, table, tail)


def shards(frames_in, in_gain, w_in, w_out, out_gain, table):
    tail = table[ROWS - REST :]
    mixed, log_total = fused(frames_in.T, in_gain[None], out_gain[None], w_in, w_out, table, tail)
    return (mixed.T, log_total.reshape(512))


def solution(mesh):
    placed = (
        P("frames", "hidden"),
        P(),
        P(None, "hidden"),
        P("hidden", None),
        P(),
        P(("frames", "hidden"), None),
    )
    return jax.shard_map(
        shards,
        mesh=mesh,
        in_specs=placed,
        out_specs=(P("frames", "hidden"), P("frames")),
        check_vma=False,
    )
```
